768 devices in a mesh: dp: 16 (over z_hi, y), expert: 48 (over z_lo, x, core).
Axes of the slice: x: 4, y: 8, z: 12 (z_hi: 2, z_lo: 6; z = z_hi * 6 + z_lo), core: 2. Of those that a mesh axis runs over, the one named last changes fastest.
Arguments:
- tokens: bfloat16 [768, 128, 1280], P(('dp', 'expert')), may hold values from -6 to 6
- slot_param: bfloat16 [1280, 48], replicated, may hold values from -0.4472136 to 0.4472136
- out_grad: bfloat16 [768, 128, 1280], P(('dp', 'expert')), may hold values from -48 to 48
- slot_outputs: bfloat16 [768, 48, 1280], P(('dp', 'expert')), may hold values from -1.5 to 1.5
- slot_inputs: bfloat16 [384, 48, 1280], P(None, 'expert'), may hold values from -6 to 6
- w_in: bfloat16 [48, 1280, 5120], P('expert', None, 'dp'), may hold values from -0.15625 to 0.15625
- w_out: bfloat16 [48, 5120, 1280], P('expert', 'dp'), may hold values from -0.078125 to 0.078125
Outputs:
- token_grad: bfloat16 [768, 128, 1280], P(('dp', 'expert'))
- w_in_grad: bfloat16 [48, 1280, 5120], P('expert', None, 'dp')
- w_out_grad: bfloat16 [48, 5120, 1280], P('expert', 'dp')
The draws below stay inside these ranges and needn't reach their ends.
All inputs are finite; a program needn't handle non-finite values.
Results may differ from the reference program's by a relative error of at most 0.034.
Values may be sent and summed in bfloat16 or wider, within the bound.
A program may use at most 32 MiB of HBM per device.

```python
import math
import jax
import jax.numpy as jnp
from jax import lax

D = 1280
FF = 5120
HALF = 128
EXPERTS = 48
PIECES = 768
IMAGES = 384
N_DP = 16


def draw_slot_param(key, part):
    key = jax.random.fold_in(key, 11)
    values = 2.5 * jax.random.truncated_normal(key, -6.0, 6.0, (D, EXPERTS), jnp.float32) / math.sqrt(D)
    return values.astype(jnp.bfloat16)


def draw_tokens(key, part):
    key = jax.random.fold_in(key, 23)
    noise_key = jax.random.fold_in(key, 0)
    values = jax.random.truncated_normal(noise_key, -6.0, 6.0, (PIECES, HALF, D), jnp.float32)
    return values.astype(jnp.bfloat16)


def shard_levels(stream_key, extent, shards, low, high):
    gain = 1.0
    for dim, blocks in shards:
        heights = jax.random.uniform(jax.random.fold_in(jax.random.fold_in(stream_key, 6), dim), (blocks,), jnp.float32, low / len(shards), high / len(shards))
        gain = gain * jnp.repeat(jnp.exp(heights), extent[dim] // blocks).reshape((-1,) + (1,) * (len(extent) - 1 - dim))
    return gain


def gaussian(rng, shape, width, bound, cuts=(), held_as=jnp.bfloat16):
    values = width * jax.random.normal(rng, shape, jnp.float32)
    if cuts:
        values = values * shard_levels(rng, shape, cuts, -0.22, 0.18)
    return jnp.clip(values, -bound, bound).astype(held_as)


def setup_inputs(seed: int = 0) -> dict:
    seeds = jax.random.split(jax.random.key(seed), 8)
    tokens = draw_tokens(jax.random.fold_in(seeds[7], 71), 0)
    slot_param = draw_slot_param(jax.random.fold_in(seeds[7], 71), 0)
    out_grad = gaussian(seeds[2], (PIECES, HALF, D), 8.0, 48.0, ((0, 768),))
    slot_outputs = gaussian(seeds[3], (PIECES, EXPERTS, D), 0.25, 1.5, ((0, 768),))
    slot_inputs = gaussian(seeds[4], (IMAGES, EXPERTS, D), 1.0, 6.0, ((1, 48),))
    w_in = gaussian(seeds[5], (EXPERTS, D, FF), D ** -0.5, 0.15625, ((0, 48), (2, 16)))
    w_out = gaussian(seeds[6], (EXPERTS, FF, D), FF ** -0.5, 0.078125, ((0, 48), (1, 16)))
    return {"tokens": tokens, "slot_param": slot_param, "out_grad": out_grad, "slot_outputs": slot_outputs, "slot_inputs": slot_inputs, "w_in": w_in, "w_out": w_out}


def gelu_pair(pre):
    normal_cdf = 0.5 * (1.0 + lax.erf(pre * 0.7071067811865476))
    normal_pdf = jnp.exp(-0.5 * pre * pre) * 0.3989422804014327
    return pre * normal_cdf, normal_cdf + pre * normal_pdf


def reference(tokens, slot_param, out_grad, slot_outputs, slot_inputs, w_in, w_out):
    f32 = jnp.float32
    bf16 = jnp.bfloat16
    image_tok = tokens.reshape(IMAGES, 2, HALF, D)
    image_grad = out_grad.reshape(IMAGES, 2, HALF, D)
    image_out = slot_outputs.reshape(IMAGES, 2, EXPERTS, D)
    param32 = slot_param.astype(f32)

    def logits_of(tok):
        return jnp.einsum('htk,ks->hts', tok.astype(f32), param32)

    def slot_side(pieces):
        tok, grad = pieces
        logits = logits_of(tok)
        combine = jax.nn.softmax(logits, axis=2)
        comb16 = combine.astype(bf16)
        partial_value = jnp.einsum('hts,htk->hsk', comb16.astype(f32), grad.astype(f32))
        slot_grad = (partial_value[0] + partial_value[1]).astype(bf16)
        col_max = jnp.max(logits, axis=1)
        col_sum = jnp.sum(jnp.exp(logits - col_max[:, None, :]), axis=1)
        top = jnp.maximum(col_max[0], col_max[1])
        total = col_sum[0] * jnp.exp(col_max[0] - top) + col_sum[1] * jnp.exp(col_max[1] - top)
        return slot_grad, top + jnp.log(total)

    slot_grad, lse = lax.map(slot_side, (image_tok, image_grad))

    def expert_side(pieces):
        inputs, grads, w_first, w_second = pieces
        pre = jnp.dot(inputs, w_first, preferred_element_type=f32)
        act, slope = gelu_pair(pre)
        act16 = act.astype(bf16)
        hid_grad = jnp.dot(grads, w_second.T, preferred_element_type=f32)
        pre_grad = (hid_grad * slope).astype(bf16)
        out_g = jnp.dot(act16.T, grads, preferred_element_type=f32).astype(bf16)
        in_g = jnp.dot(inputs.T, pre_grad, preferred_element_type=f32).astype(bf16)
        group = FF // N_DP
        terms = jnp.einsum('grf,krf->rgk', pre_grad.reshape(IMAGES, N_DP, group).astype(f32),
                           w_first.reshape(D, N_DP, group).astype(f32))
        terms = lax.optimization_barrier(terms.astype(bf16)).astype(f32)
        slot_in = jnp.sum(terms, axis=0).astype(bf16)
        slot_dot = jnp.sum(inputs.astype(f32) * slot_in.astype(f32), axis=1)
        return in_g, out_g, slot_in, slot_dot

    w_in_grad, w_out_grad, slot_in, slot_dot = lax.map(
        expert_side,
        (jnp.transpose(slot_inputs, (1, 0, 2)), jnp.transpose(slot_grad, (1, 0, 2)), w_in, w_out))
    slot_in = jnp.transpose(slot_in, (1, 0, 2))
    slot_dot = jnp.transpose(slot_dot, (1, 0))

    def token_side(pieces):
        tok, grad, outputs, norm_log, in_grad, dot_term = pieces
        logits = logits_of(tok)
        combine = jax.nn.softmax(logits, axis=2)
        dispatch = jnp.exp(logits - norm_log[None, None, :])
        disp16 = dispatch.astype(bf16)
        in32 = in_grad.astype(f32)
        disp_grad = jnp.einsum('htk,sk->hts', tok.astype(f32), in32)
        comb_grad = jnp.einsum('htk,hsk->hts', grad.astype(f32), outputs.astype(f32))
        row_term = jnp.sum(combine * comb_grad, axis=2, keepdims=True)
        logit_grad = (combine * (comb_grad - row_term)
                      + dispatch * (disp_grad - dot_term[None, None, :])).astype(bf16)
        result = jnp.einsum('hts,sk->htk', disp16.astype(f32), in32)
        result = result + jnp.einsum('hts,ks->htk', logit_grad.astype(f32), param32)
        return result.astype(bf16)

    token_grad = lax.map(token_side, (image_tok, image_grad, image_out, lse, slot_in, slot_dot))
    return token_grad.reshape(PIECES, HALF, D), w_in_grad, w_out_grad
```

```python
import jax
import jax.numpy as jnp
from jax import lax
from jax.experimental import pallas as pl
from jax.experimental.pallas import tpu as pltpu
from jax.sharding import PartitionSpec as P

F32 = jnp.float32
BF16 = jnp.bfloat16
MESH = pl.DeviceIdType.MESH

RING = 8
HALVES = 2
CHIPS = 24
BLOCK = HALVES * CHIPS
PIECE = 16
LANES = 128


def matmul(a, b):
    return lax.dot_general(a, b, (((1,), (0,)), ((), ())), preferred_element_type=F32)


def matmul_t(a, b):
    return lax.dot_general(a, b, (((1,), (1,)), ((), ())), preferred_element_type=F32)


def gelu_pair(pre):
    normal_cdf = 0.5 * (1.0 + lax.erf(pre * 0.7071067811865476))
    normal_pdf = jnp.exp(-0.5 * pre * pre) * 0.3989422804014327
    return pre * normal_cdf, normal_cdf + pre * normal_pdf


def kernel(
    tok_in, param_in, ograd_in, sout_in, x_in, win_in, wout_in,
    tok_grad, win_grad, wout_grad,
    tok, param, ograd, sout, x, win, wout,
    param_p, xp, slope, act_t, grads, pgs, pg_t, sums,
    part, pair_part, lse_own, lse_pair, disp, base,
    tiles, out_a, in_a, out_b, in_b, back,
    rs_out_r, rs_out_l, rs_in_r, rs_in_l,
    local_sem, pair_send, pair_recv, all_send, all_recv, all_self,
    ag_send, ag_recv, rs_send, rs_recv,
):
    width = tok.shape[1]
    half = width // 2
    cuts = width // LANES
    d = lax.axis_index("dp")
    e = lax.axis_index("expert")
    zh, y = d // RING, d % RING
    chip, core = e // 2, e % 2
    me = zh * CHIPS + chip
    other = (d, e + 1 - 2 * core)
    right = (zh * RING + (y + 1) % RING, e)
    left = (zh * RING + (y + RING - 1) % RING, e)

    def peer(n):
        t = (me + n) % BLOCK
        return t, t % CHIPS, ((t // CHIPS) * RING + y, 2 * (t % CHIPS) + core)

    loads = [
        pltpu.make_async_copy(src, dst, local_sem.at[i])
        for i, (src, dst) in enumerate(
            [(tok_in, tok), (param_in, param), (ograd_in, ograd), (x_in, x),
             (win_in, win), (sout_in, sout), (wout_in, wout)]
        )
    ]
    for load in loads:
        load.start()

    barrier = pltpu.get_barrier_semaphore()
    for device in (other, left, right):
        pl.semaphore_signal(barrier, inc=1, device_id=device, device_id_type=MESH)

    @pl.loop(1, BLOCK)
    def _(n):
        _, _, device = peer(n)
        pl.semaphore_signal(barrier, inc=1, device_id=device, device_id_type=MESH)

    row = lax.broadcasted_iota(jnp.int32, (BLOCK, BLOCK), 0)
    col = lax.broadcasted_iota(jnp.int32, (BLOCK, BLOCK), 1)
    wanted = jnp.where(row < CHIPS, 2 * row, 2 * (row - CHIPS) + 1)
    perm = jnp.where(col == wanted, 1.0, 0.0).astype(BF16)
    loads[0].wait()
    loads[1].wait()
    param_p[...] = matmul(perm, param[...]).astype(BF16)
    logits = matmul_t(param_p[...], tok[...])
    ex = jnp.exp(logits - jnp.max(logits, axis=0, keepdims=True))
    combine = ex / jnp.sum(ex, axis=0, keepdims=True)
    loads[2].wait()
    part[...] = matmul(combine.astype(BF16), ograd[...])
    col_max = jnp.max(logits, axis=1, keepdims=True)
    col_sum = jnp.sum(jnp.exp(logits - col_max), axis=1, keepdims=True)
    lse_own[...] = jnp.broadcast_to(col_max + jnp.log(col_sum), lse_own.shape)

    pl.semaphore_wait(barrier, BLOCK - 1 + 3)
    mine = pl.ds(pl.multiple_of(CHIPS * core, 8), CHIPS)
    theirs = pl.ds(pl.multiple_of(CHIPS * (1 - core), 8), CHIPS)
    send_part = pltpu.make_async_remote_copy(
        part.at[theirs], pair_part, pair_send.at[0], pair_recv.at[0], device_id=other, device_id_type=MESH
    )
    send_part.start()
    send_lse = pltpu.make_async_remote_copy(
        lse_own, lse_pair, pair_send.at[1], pair_recv.at[1], device_id=other, device_id_type=MESH
    )
    send_lse.start()

    tiles[...] = jnp.zeros_like(tiles)
    send_part.wait_recv()
    slot_sum = (part[mine, :] + pair_part[...]).astype(BF16).astype(F32)
    for i in range(cuts):
        tiles[pl.ds(i, CHIPS, stride=PIECE), :] = slot_sum[:, i * LANES:(i + 1) * LANES]
    out_a[...] = tiles[pl.ds(0, CHIPS * PIECE), :].astype(BF16)

    def piece(ref, i):
        return ref.at[pl.ds(pl.multiple_of(i * PIECE, PIECE), PIECE)]

    all_but_one = pl.ds(0, (BLOCK - 1) * PIECE)

    @pl.loop(1, BLOCK)
    def _(n):
        _, owner, device = peer(n)
        pltpu.make_async_remote_copy(
            piece(out_a, owner), piece(in_a, me), all_send.at[0], all_recv.at[0],
            device_id=device, device_id_type=MESH,
        ).start()

    self_a = pltpu.make_async_copy(piece(out_a, chip), piece(in_a, me), all_self.at[0])
    self_a.start()

    loads[3].wait()
    for b in range(RING):
        lo = x[b * CHIPS:(b + 1) * CHIPS, :]
        hi = x[(RING + b) * CHIPS:(RING + b + 1) * CHIPS, :]
        xp[b * BLOCK:(b + 1) * BLOCK, :] = jnp.concatenate([lo, hi], axis=0)
    loads[4].wait()
    for i in range(xp.shape[0] // LANES):
        rows = slice(i * LANES, (i + 1) * LANES)
        act, rise = gelu_pair(matmul_t(xp[rows, :], win[...]))
        slope[rows, :] = rise
        act_t[:, rows] = act.T.astype(BF16)
    loads[5].wait()
    comb_grad = matmul_t(matmul(perm, sout[...]).astype(BF16), ograd[...])
    base[...] = combine * (comb_grad - jnp.sum(combine * comb_grad, axis=0, keepdims=True))
    send_lse.wait_recv()
    lse_a, lse_b = lse_own[...], lse_pair[...]
    top = jnp.maximum(lse_a, lse_b)
    lse = top + jnp.log(jnp.exp(lse_a - top) + jnp.exp(lse_b - top))
    disp[...] = jnp.exp(logits - lse)

    def rows_of(b):
        return pl.ds(pl.multiple_of(b * BLOCK, PIECE), BLOCK)

    pltpu.make_async_copy(in_a.at[all_but_one], in_a.at[all_but_one], all_recv.at[0]).wait()
    self_a.wait()
    tiles[...] = in_a[...].astype(F32)
    for i in range(cuts):
        grads[rows_of(y), i * LANES:(i + 1) * LANES] = tiles[pl.ds(i, BLOCK, stride=PIECE), :].astype(BF16)
    loads[6].wait()

    def work(blocks):
        g = [grads[rows_of(b), :] for b in blocks]
        s = [slope[rows_of(b), :] for b in blocks]
        g = g[0] if len(g) == 1 else jnp.concatenate(g, axis=0)
        s = s[0] if len(s) == 1 else jnp.concatenate(s, axis=0)
        pg = (matmul_t(g, wout[...]) * s).astype(BF16)
        total = matmul(pg, win[...])
        for i, b in enumerate(blocks):
            pgs[rows_of(b), :] = pg[i * BLOCK:(i + 1) * BLOCK, :]
            sums[rows_of(b), :] = total[i * BLOCK:(i + 1) * BLOCK, :]

    def at(offset):
        return (y + offset + RING) % RING

    lanes_r, lanes_l = pl.ds(0, half), pl.ds(half, half)
    ag = []
    for s in range(4):
        to_r = grads.at[rows_of(at(-s))]
        to_l = grads.at[rows_of(at(s))]
        if s == 3:
            to_r = grads.at[rows_of(at(-s)), lanes_r]
            to_l = grads.at[rows_of(at(s)), lanes_l]
        pair = [
            pltpu.make_async_remote_copy(
                ref, ref, ag_send.at[s, i], ag_recv.at[s, i], device_id=device, device_id_type=MESH
            )
            for i, (ref, device) in enumerate(((to_r, right), (to_l, left)))
        ]
        for copy in pair:
            copy.start()
        work([at(0)] if s == 0 else [at(-s), at(s)])
        for copy in pair:
            copy.wait_recv()
        ag += pair
    work([at(4)])

    rs = []
    chunk = 2 * LANES

    def weight_out():
        for i in range(width // chunk):
            lanes = slice(i * chunk, (i + 1) * chunk)
            wout_grad[:, lanes] = matmul(act_t[...], grads[:, lanes]).astype(BF16)

    def transpose_pg():
        for i in range(pgs.shape[0] // LANES):
            rows = slice(i * LANES, (i + 1) * LANES)
            pg_t[:, rows] = pgs[rows, :].astype(F32).T.astype(BF16)

    def weight_in():
        for i in range(width // chunk):
            lanes = slice(i * chunk, (i + 1) * chunk)
            win_grad[:, lanes] = matmul(pg_t[...], xp[:, lanes]).astype(BF16)

    beside = (weight_out, transpose_pg, weight_in, lambda: None)
    for s in range(4):
        dest_r, dest_l = rows_of(at(4 - s)), rows_of(at(s - 4))
        if s == 0:
            rs_out_r[0] = sums[dest_r, :].astype(BF16)
            moves = (
                (rs_out_r.at[0, :, lanes_r], rs_in_r.at[0, :, lanes_r], right),
                (rs_out_r.at[0, :, lanes_l], rs_in_l.at[0, :, lanes_l], left),
            )
        else:
            if s == 1:
                rs_out_r[s, :, :half] = (sums[dest_r, :half] + rs_in_r[0, :, :half].astype(F32)).astype(BF16)
                rs_out_r[s, :, half:] = sums[dest_r, half:].astype(BF16)
                rs_out_l[s, :, :half] = sums[dest_l, :half].astype(BF16)
                rs_out_l[s, :, half:] = (sums[dest_l, half:] + rs_in_l[0, :, half:].astype(F32)).astype(BF16)
            else:
                rs_out_r[s] = (sums[dest_r, :] + rs_in_r[s - 1].astype(F32)).astype(BF16)
                rs_out_l[s] = (sums[dest_l, :] + rs_in_l[s - 1].astype(F32)).astype(BF16)
            moves = (
                (rs_out_r.at[s], rs_in_r.at[s], right),
                (rs_out_l.at[s], rs_in_l.at[s], left),
            )
        pair = [
            pltpu.make_async_remote_copy(
                src, dst, rs_send.at[s, i], rs_recv.at[s, i], device_id=device, device_id_type=MESH
            )
            for i, (src, dst, device) in enumerate(moves)
        ]
        for copy in pair:
            copy.start()
        beside[s]()
        for copy in pair:
            copy.wait_recv()
        rs += pair

    total = (sums[rows_of(y), :] + rs_in_r[3].astype(F32) + rs_in_l[3].astype(F32)).astype(BF16).astype(F32)
    dot = jnp.sum(xp[rows_of(y), :].astype(F32) * total, axis=1, keepdims=True)
    dot_hi = dot.astype(BF16).astype(F32)
    for i in range(cuts):
        tiles[pl.ds(i, BLOCK, stride=PIECE), :] = total[:, i * LANES:(i + 1) * LANES]
    tiles[pl.ds(cuts, BLOCK, stride=PIECE), :] = jnp.broadcast_to(dot_hi, (BLOCK, LANES))
    tiles[pl.ds(cuts + 1, BLOCK, stride=PIECE), :] = jnp.broadcast_to(dot - dot_hi, (BLOCK, LANES))
    out_b[...] = tiles[...].astype(BF16)

    @pl.loop(1, BLOCK)
    def _(n):
        t, _, device = peer(n)
        pltpu.make_async_remote_copy(
            piece(out_b, t), piece(in_b, me), all_send.at[1], all_recv.at[1],
            device_id=device, device_id_type=MESH,
        ).start()

    self_b = pltpu.make_async_copy(piece(out_b, me), piece(in_b, me), all_self.at[1])
    self_b.start()
    pltpu.make_async_copy(in_b.at[all_but_one], in_b.at[all_but_one], all_recv.at[1]).wait()
    self_b.wait()

    tiles[...] = in_b[...].astype(F32)

    def both(i):
        v = tiles[pl.ds(i, BLOCK, stride=PIECE), :]
        return v[:CHIPS, :] + v[CHIPS:, :]

    for i in range(cuts):
        back[mine, i * LANES:(i + 1) * LANES] = both(i)
    back[mine, width:width + LANES] = both(cuts) + both(cuts + 1)
    send_back = pltpu.make_async_remote_copy(
        back.at[mine], back.at[mine], pair_send.at[2], pair_recv.at[2], device_id=other, device_id_type=MESH
    )
    send_back.start()
    send_back.wait_recv()

    in_grad = back[:, :width].astype(BF16)
    disp_grad = matmul_t(in_grad, tok[...])
    logit_grad = base[...] + disp[...] * (disp_grad - back[:, width:width + LANES])
    left_t = jnp.concatenate([disp[...], logit_grad], axis=0).T.astype(BF16)
    tok_grad[...] = matmul(left_t, jnp.concatenate([in_grad, param_p[...]], axis=0)).astype(BF16)

    send_part.wait_send()
    send_lse.wait_send()
    send_back.wait_send()
    for i in range(2):
        pltpu.make_async_copy(in_b.at[all_but_one], in_b.at[all_but_one], all_send.at[i]).wait()
    for copy in ag + rs:
        copy.wait_send()


def body(tokens, slot_param, out_grad, slot_outputs, slot_inputs, w_in, w_out):
    tok, ograd, sout = tokens[0], out_grad[0], slot_outputs[0]
    x = slot_inputs[:, 0]
    param = slot_param.T
    win, wout = w_in[0].T, w_out[0]
    images, width = x.shape
    hidden = wout.shape[0]
    slots = param.shape[0]
    tokens_here = tok.shape[0]
    vm = pltpu.VMEM
    dma = pltpu.SemaphoreType.DMA
    any_space = pl.BlockSpec(memory_space=pl.ANY)
    vmem = pl.BlockSpec(memory_space=pltpu.VMEM)
    tok_grad, win_grad, wout_grad = pl.pallas_call(
        kernel,
        out_shape=(
            jax.ShapeDtypeStruct((tokens_here, width), BF16),
            jax.ShapeDtypeStruct((hidden, width), BF16),
            jax.ShapeDtypeStruct((hidden, width), BF16),
        ),
        in_specs=[any_space] * 7,
        out_specs=(vmem, vmem, vmem),
        scratch_shapes=[
            vm((tokens_here, width), BF16), vm((slots, width), BF16), vm((tokens_here, width), BF16),
            vm((slots, width), BF16), vm((images, width), BF16), vm((hidden, width), BF16),
            vm((hidden, width), BF16),
            vm((slots, width), BF16), vm((images, width), BF16), vm((images, hidden), F32),
            vm((hidden, images), BF16), vm((images, width), BF16), vm((images, hidden), BF16),
            vm((hidden, images), BF16), vm((images, width), F32),
            vm((slots, width), F32), vm((CHIPS, width), F32), vm((slots, LANES), F32),
            vm((slots, LANES), F32), vm((slots, LANES), F32), vm((slots, LANES), F32),
            vm((BLOCK * PIECE, LANES), F32), vm((CHIPS * PIECE, LANES), BF16),
            vm((BLOCK * PIECE, LANES), BF16), vm((BLOCK * PIECE, LANES), BF16),
            vm((BLOCK * PIECE, LANES), BF16), vm((slots, width + LANES), F32),
            vm((4, BLOCK, width), BF16), vm((4, BLOCK, width), BF16),
            vm((4, BLOCK, width), BF16), vm((4, BLOCK, width), BF16),
            dma((7,)), dma((3,)), dma((3,)), dma((2,)), dma((2,)), dma((2,)),
            dma((4, 2)), dma((4, 2)), dma((4, 2)), dma((4, 2)),
        ],
        compiler_params=pltpu.CompilerParams(
            collective_id=0, has_side_effects=True, vmem_limit_bytes=40 * 1024 * 1024
        ),
    )(tok, param, ograd, sout, x, win, wout)
    return tok_grad[None], win_grad.T[None], wout_grad[None]


def solution(mesh):
    placed = (
        P(("dp", "expert"), None, None),
        P(),
        P(("dp", "expert"), None, None),
        P(("dp", "expert"), None, None),
        P(None, "expert", None),
        P("expert", None, "dp"),
        P("expert", "dp", None),
    )
    return jax.shard_map(
        body,
        mesh=mesh,
        in_specs=placed,
        out_specs=(
            P(("dp", "expert"), None, None),
            P("expert", None, "dp"),
            P("expert", "dp", None),
        ),
        check_vma=False,
    )
```

```python
import jax
import jax.numpy as jnp
from jax import lax
from jax.experimental import pallas as pl
from jax.experimental.pallas import tpu as pltpu
from jax.sharding import PartitionSpec as P

F32 = jnp.float32
BF16 = jnp.bfloat16
MESH = pl.DeviceIdType.MESH

RING = 8
HALVES = 2
CHIPS = 24
BLOCK = HALVES * CHIPS
PIECE = 16
LANES = 128
PARTS = ((0, 384), (384, 256), (640, 384), (1024, 256))
OPPOSITE = ((0, 1), (2, 3))


def matmul(a, b):
    return lax.dot_general(a, b, (((1,), (0,)), ((), ())), preferred_element_type=F32)


def matmul_t(a, b):
    return lax.dot_general(a, b, (((1,), (1,)), ((), ())), preferred_element_type=F32)


def gelu_pair(pre):
    normal_cdf = 0.5 * (1.0 + lax.erf(pre * 0.7071067811865476))
    normal_pdf = jnp.exp(-0.5 * pre * pre) * 0.3989422804014327
    return pre * normal_cdf, normal_cdf + pre * normal_pdf


def kernel(
    tok_in, param_in, ograd_in, sout_in, x_in, win_in, wout_in,
    win_out, wout_out, tok, param_p, base, disp, back,
    param, ograd, sout, x, win, wout,
    xp, slope, act_t, grads, pgs, pg_t, sums,
    part, pair_part, lse_own, lse_pair,
    tiles, out_a, in_a, out_b, in_b,
    rs_out, rs_in, out_part,
    local_sem, pair_send, pair_recv, all_send, all_recv, all_self,
    ag_send, ag_recv, rs_send, rs_recv,
):
    width = tok.shape[1]
    cuts = width // LANES
    d = lax.axis_index("dp")
    e = lax.axis_index("expert")
    zh, y = d // RING, d % RING
    chip, core = e // 2, e % 2
    me = zh * CHIPS + chip
    other = (d, e + 1 - 2 * core)
    right = (zh * RING + (y + 1) % RING, e)
    left = (zh * RING + (y + RING - 1) % RING, e)

    def peer(n):
        t = (me + CHIPS + n) % BLOCK
        return t, t % CHIPS, ((t // CHIPS) * RING + y, 2 * (t % CHIPS) + core)

    def for_peers(act):
        pl.loop(0, CHIPS)(act)
        pl.loop(CHIPS + 1, BLOCK)(act)

    loads = [
        pltpu.make_async_copy(src, dst, local_sem.at[i])
        for i, (src, dst) in enumerate(
            [(tok_in, tok), (param_in, param), (ograd_in, ograd), (x_in, x),
             (win_in, win), (sout_in, sout), (wout_in, wout)]
        )
    ]
    for load in loads[:3]:
        load.start()

    barrier = pltpu.get_barrier_semaphore()

    def greet(n):
        _, _, device = peer(n)
        pl.semaphore_signal(barrier, inc=1, device_id=device, device_id_type=MESH)

    for_peers(greet)
    for device in (other, left, right):
        pl.semaphore_signal(barrier, inc=1, device_id=device, device_id_type=MESH)

    def softmax(logits):
        ex = jnp.exp(logits - jnp.max(logits, axis=0, keepdims=True))
        return ex / jnp.sum(ex, axis=0, keepdims=True)

    loads[0].wait()
    loads[1].wait()
    combine = softmax(matmul_t(param[...], tok[...]))
    loads[2].wait()
    whole = matmul(combine.astype(BF16), ograd[...])
    for i in range(cuts):
        part[i] = whole[:, i * LANES:(i + 1) * LANES]
        out_part[i] = part[i, pl.ds(1 - core, CHIPS, stride=2), :]
    for load in loads[3:]:
        load.start()
    tiles[...] = jnp.zeros_like(tiles)

    pl.semaphore_wait(barrier, BLOCK - 1 + 3)
    send_part = pltpu.make_async_remote_copy(
        out_part, pair_part, pair_send.at[0], pair_recv.at[0], device_id=other, device_id_type=MESH
    )
    send_part.start()
    send_part.wait_recv()
    for i in range(cuts):
        tiles[pl.ds(i, CHIPS, stride=PIECE), :] = part[i, pl.ds(core, CHIPS, stride=2), :] + pair_part[i]
    out_a[...] = tiles[pl.ds(0, CHIPS * PIECE), :].astype(BF16)

    def piece(ref, i):
        return ref.at[pl.ds(pl.multiple_of(i * PIECE, PIECE), PIECE)]

    all_but_one = pl.ds(0, (BLOCK - 1) * PIECE)

    def give_a(n):
        _, owner, device = peer(n)
        pltpu.make_async_remote_copy(
            piece(out_a, owner), piece(in_a, me), all_send.at[0], all_recv.at[0],
            device_id=device, device_id_type=MESH,
        ).start()

    for_peers(give_a)
    self_a = pltpu.make_async_copy(piece(out_a, chip), piece(in_a, me), all_self.at[0])
    self_a.start()

    mine = pl.ds(pl.multiple_of(CHIPS * core, 8), CHIPS)
    row = lax.broadcasted_iota(jnp.int32, (BLOCK, BLOCK), 0)
    col = lax.broadcasted_iota(jnp.int32, (BLOCK, BLOCK), 1)
    wanted = jnp.where(row < CHIPS, 2 * row, 2 * (row - CHIPS) + 1)
    perm = jnp.where(col == wanted, 1.0, 0.0).astype(BF16)
    param_p[...] = matmul(perm, param[...]).astype(BF16)
    logits = matmul_t(param_p[...], tok[...])
    combine = softmax(logits)
    col_max = jnp.max(logits, axis=1, keepdims=True)
    col_sum = jnp.sum(jnp.exp(logits - col_max), axis=1, keepdims=True)
    lse_own[...] = jnp.broadcast_to(col_max + jnp.log(col_sum), lse_own.shape)
    send_lse = pltpu.make_async_remote_copy(
        lse_own, lse_pair, pair_send.at[1], pair_recv.at[1], device_id=other, device_id_type=MESH
    )
    send_lse.start()
    loads[3].wait()
    for b in range(RING):
        lo = x[b * CHIPS:(b + 1) * CHIPS, :]
        hi = x[(RING + b) * CHIPS:(RING + b + 1) * CHIPS, :]
        xp[b * BLOCK:(b + 1) * BLOCK, :] = jnp.concatenate([lo, hi], axis=0)
    loads[4].wait()
    for i in range(xp.shape[0] // LANES):
        rows = slice(i * LANES, (i + 1) * LANES)
        act, rise = gelu_pair(matmul_t(xp[rows, :], win[...]))
        slope[rows, :] = rise
        act_t[:, rows] = act.T.astype(BF16)
    loads[5].wait()
    comb_grad = matmul_t(matmul(perm, sout[...]).astype(BF16), ograd[...])
    base[...] = combine * (comb_grad - jnp.sum(combine * comb_grad, axis=0, keepdims=True))
    send_lse.wait_recv()
    lse_a, lse_b = lse_own[...], lse_pair[...]
    top = jnp.maximum(lse_a, lse_b)
    lse = top + jnp.log(jnp.exp(lse_a - top) + jnp.exp(lse_b - top))
    disp[...] = jnp.exp(logits - lse)

    def rows_of(b):
        return pl.ds(pl.multiple_of(b * BLOCK, PIECE), BLOCK)

    pltpu.make_async_copy(in_a.at[all_but_one], in_a.at[all_but_one], all_recv.at[0]).wait()
    self_a.wait()
    tiles[...] = in_a[...].astype(F32)
    for i in range(cuts):
        grads[rows_of(y), i * LANES:(i + 1) * LANES] = tiles[pl.ds(i, BLOCK, stride=PIECE), :].astype(BF16)
    loads[6].wait()

    def work(blocks):
        g = [grads[rows_of(b), :] for b in blocks]
        s = [slope[rows_of(b), :] for b in blocks]
        g = g[0] if len(g) == 1 else jnp.concatenate(g, axis=0)
        s = s[0] if len(s) == 1 else jnp.concatenate(s, axis=0)
        pg = (matmul_t(g, wout[...]) * s).astype(BF16)
        total = matmul(pg, win[...])
        for i, b in enumerate(blocks):
            pgs[rows_of(b), :] = pg[i * BLOCK:(i + 1) * BLOCK, :]
            sums[rows_of(b), :] = total[i * BLOCK:(i + 1) * BLOCK, :]

    def at(offset):
        return (y + offset + RING) % RING

    sides = (right, left)
    ag = {}
    for s in range(4):
        for i in range(2):
            rows = rows_of(at(-s if i == 0 else s))
            for c in OPPOSITE[i] if s == 3 else range(4):
                ref = grads.at[rows, pl.ds(*PARTS[c])]
                ag[s, i, c] = pltpu.make_async_remote_copy(
                    ref, ref, ag_send.at[s, i, c], ag_recv.at[s, i, c],
                    device_id=sides[i], device_id_type=MESH,
                )
    for c in range(4):
        for i in range(2):
            ag[0, i, c].start()
    work([at(0)])
    for s in range(1, 4):
        for c in (0, 2, 1, 3):
            for i in range(2):
                ag[s - 1, i, c].wait_recv()
                if (s, i, c) in ag:
                    ag[s, i, c].start()
        work([at(-s), at(s)])
    for i in range(2):
        for c in OPPOSITE[i]:
            ag[3, i, c].wait_recv()
    work([at(4)])

    chunk = 2 * LANES

    def weight_out():
        for i in range(width // chunk):
            lanes = slice(i * chunk, (i + 1) * chunk)
            wout_out[:, lanes] = matmul(act_t[...], grads[:, lanes]).astype(BF16)

    def transpose_pg():
        for i in range(pgs.shape[0] // LANES):
            rows = slice(i * LANES, (i + 1) * LANES)
            pg_t[:, rows] = pgs[rows, :].astype(F32).T.astype(BF16)

    def weight_in(first, last):
        for i in range(first, last):
            lanes = slice(i * chunk, (i + 1) * chunk)
            win_out[:, lanes] = matmul(pg_t[...], xp[:, lanes]).astype(BF16)

    rs = {}

    def give_sum(s, i, c):
        dest = rows_of(at(4 - s if i == 0 else s - 4))
        lanes = pl.ds(*PARTS[c])
        term = sums[dest, lanes]
        if (s - 1, i, c) in rs:
            rs[s - 1, i, c].wait_recv()
            term = term + rs_in[s - 1, i, :, lanes].astype(F32)
        rs_out[s, i, :, lanes] = term.astype(BF16)
        rs[s, i, c] = pltpu.make_async_remote_copy(
            rs_out.at[s, i, :, lanes], rs_in.at[s, i, :, lanes], rs_send.at[s, i, c], rs_recv.at[s, i, c],
            device_id=sides[i], device_id_type=MESH,
        )
        rs[s, i, c].start()

    def give_sums(s, late):
        for k in range(2):
            for i in range(2):
                give_sum(s, i, OPPOSITE[i if late else 1 - i][k])

    give_sums(0, True)
    give_sums(1, False)
    weight_out()
    transpose_pg()
    give_sums(1, True)
    give_sums(2, False)
    weight_in(0, 2)
    give_sums(2, True)
    give_sums(3, False)
    weight_in(2, 5)
    give_sums(3, True)
    for i in range(2):
        for c in range(4):
            rs[3, i, c].wait_recv()

    total = (sums[rows_of(y), :] + rs_in[3, 0].astype(F32) + rs_in[3, 1].astype(F32)).astype(BF16).astype(F32)
    dot = jnp.sum(xp[rows_of(y), :].astype(F32) * total, axis=1, keepdims=True)
    dot_hi = dot.astype(BF16).astype(F32)
    for i in range(cuts):
        tiles[pl.ds(i, BLOCK, stride=PIECE), :] = total[:, i * LANES:(i + 1) * LANES]
    tiles[pl.ds(cuts, BLOCK, stride=PIECE), :] = jnp.broadcast_to(dot_hi, (BLOCK, LANES))
    tiles[pl.ds(cuts + 1, BLOCK, stride=PIECE), :] = jnp.broadcast_to(dot - dot_hi, (BLOCK, LANES))
    out_b[...] = tiles[...].astype(BF16)

    def give_b(n):
        t, _, device = peer(n)
        pltpu.make_async_remote_copy(
            piece(out_b, t), piece(in_b, me), all_send.at[1], all_recv.at[1],
            device_id=device, device_id_type=MESH,
        ).start()

    for_peers(give_b)
    self_b = pltpu.make_async_copy(piece(out_b, me), piece(in_b, me), all_self.at[1])
    self_b.start()
    pltpu.make_async_copy(in_b.at[all_but_one], in_b.at[all_but_one], all_recv.at[1]).wait()
    self_b.wait()

    tiles[...] = in_b[...].astype(F32)

    def both(i):
        v = tiles[pl.ds(i, BLOCK, stride=PIECE), :]
        return v[:CHIPS, :] + v[CHIPS:, :]

    for i in range(cuts):
        back[mine, i * LANES:(i + 1) * LANES] = both(i)
    back[mine, width:width + LANES] = both(cuts) + both(cuts + 1)
    send_back = pltpu.make_async_remote_copy(
        back.at[mine], back.at[mine], pair_send.at[2], pair_recv.at[2], device_id=other, device_id_type=MESH
    )
    send_back.start()
    send_back.wait_recv()

    send_part.wait_send()
    send_lse.wait_send()
    send_back.wait_send()
    for i in range(2):
        pltpu.make_async_copy(in_b.at[all_but_one], in_b.at[all_but_one], all_send.at[i]).wait()
    for copy in list(ag.values()) + list(rs.values()):
        copy.wait_send()


def finish(win_made, wout_made, tok, param_p, base, disp, back, tok_grad, win_grad, wout_grad, tok_out, sem):
    width = tok.shape[1]
    stores = [
        pltpu.make_async_copy(win_made, win_grad, sem.at[0]),
        pltpu.make_async_copy(wout_made, wout_grad, sem.at[1]),
    ]
    for store in stores:
        store.start()
    in_grad = back[:, :width].astype(BF16)
    disp_grad = matmul_t(in_grad, tok[...])
    logit_grad = base[...] + disp[...] * (disp_grad - back[:, width:width + LANES])
    left_t = jnp.concatenate([disp[...], logit_grad], axis=0).T.astype(BF16)
    half = width // 2
    for i in range(2):
        lanes = slice(i * half, (i + 1) * half)
        right_t = jnp.concatenate([in_grad[:, lanes], param_p[:, lanes]], axis=0)
        tok_out[:, lanes] = matmul(left_t, right_t).astype(BF16)
        store = pltpu.make_async_copy(tok_out.at[:, lanes], tok_grad.at[:, lanes], sem.at[2 + i])
        store.start()
        stores.append(store)
    for store in stores:
        store.wait()


def body(tokens, slot_param, out_grad, slot_outputs, slot_inputs, w_in, w_out):
    tok, ograd, sout = tokens[0], out_grad[0], slot_outputs[0]
    x = slot_inputs[:, 0]
    param = slot_param.T
    win, wout = w_in[0].T, w_out[0]
    images, width = x.shape
    hidden = wout.shape[0]
    slots = param.shape[0]
    tokens_here = tok.shape[0]
    vm = pltpu.VMEM
    dma = pltpu.SemaphoreType.DMA
    hbm = pl.BlockSpec(memory_space=pltpu.HBM)
    args = [pltpu.with_memory_space_constraint(v, pltpu.HBM) for v in (tok, param, ograd, sout, x, win, wout)]
    in_vmem = pl.BlockSpec(memory_space=pltpu.VMEM)
    made = pl.pallas_call(
        kernel,
        out_shape=(
            vm((hidden, width), BF16), vm((hidden, width), BF16), vm((tokens_here, width), BF16),
            vm((slots, width), BF16), vm((slots, LANES), F32), vm((slots, LANES), F32),
            vm((slots, width + LANES), F32),
        ),
        in_specs=[hbm] * 7,
        out_specs=(in_vmem,) * 7,
        scratch_shapes=[
            vm((slots, width), BF16), vm((tokens_here, width), BF16),
            vm((slots, width), BF16), vm((images, width), BF16), vm((hidden, width), BF16),
            vm((hidden, width), BF16),
            vm((images, width), BF16), vm((images, hidden), F32),
            vm((hidden, images), BF16), vm((images, width), BF16), vm((images, hidden), BF16),
            vm((hidden, images), BF16), vm((images, width), F32),
            vm((width // LANES, slots, LANES), F32), vm((width // LANES, CHIPS, LANES), F32),
            vm((slots, LANES), F32), vm((slots, LANES), F32),
            vm((BLOCK * PIECE, LANES), F32), vm((CHIPS * PIECE, LANES), BF16),
            vm((BLOCK * PIECE, LANES), BF16), vm((BLOCK * PIECE, LANES), BF16),
            vm((BLOCK * PIECE, LANES), BF16),
            vm((4, 2, BLOCK, width), BF16), vm((4, 2, BLOCK, width), BF16),
            vm((width // LANES, CHIPS, LANES), F32),
            dma((7,)), dma((3,)), dma((3,)), dma((2,)), dma((2,)), dma((2,)),
            dma((4, 2, 4)), dma((4, 2, 4)), dma((4, 2, 4)), dma((4, 2, 4)),
        ],
        compiler_params=pltpu.CompilerParams(
            collective_id=0, has_side_effects=True, vmem_limit_bytes=40 * 1024 * 1024
        ),
    )(*args)
    tok_grad, win_grad, wout_grad = pl.pallas_call(
        finish,
        out_shape=(
            jax.ShapeDtypeStruct((tokens_here, width), BF16),
            jax.ShapeDtypeStruct((hidden, width), BF16),
            jax.ShapeDtypeStruct((hidden, width), BF16),
        ),
        in_specs=[in_vmem] * 7,
        out_specs=(hbm,) * 3,
        scratch_shapes=[vm((tokens_here, width), BF16), dma((4,))],
        compiler_params=pltpu.CompilerParams(vmem_limit_bytes=32 * 1024 * 1024),
    )(*made)
    return tok_grad[None], win_grad.T[None], wout_grad[None]


def solution(mesh):
    placed = (
        P(("dp", "expert"), None, None),
        P(),
        P(("dp", "expert"), None, None),
        P(("dp", "expert"), None, None),
        P(None, "expert", None),
        P("expert", None, "dp"),
        P("expert", "dp", None),
    )
    return jax.shard_map(
        body,
        mesh=mesh,
        in_specs=placed,
        out_specs=(
            P(("dp", "expert"), None, None),
            P("expert", None, "dp"),
            P("expert", "dp", None),
        ),
        check_vma=False,
    )
```

```python
import jax
import jax.numpy as jnp
from jax import lax
from jax.experimental import pallas as pl
from jax.experimental.pallas import tpu as pltpu
from jax.sharding import PartitionSpec as P

F32 = jnp.float32
BF16 = jnp.bfloat16
MESH = pl.DeviceIdType.MESH

RING = 8
HALVES = 2
ROW = 4
CHIPS = 24
BLOCK = HALVES * CHIPS
ALIGN = 16
LANES = 128
PARTS = ((0, 384), (384, 256), (640, 384), (1024, 256))
OPPOSITE = ((0, 1), (2, 3))


def matmul(a, b):
    return lax.dot_general(a, b, (((1,), (0,)), ((), ())), preferred_element_type=F32)


def matmul_t(a, b):
    return lax.dot_general(a, b, (((1,), (1,)), ((), ())), preferred_element_type=F32)


def gelu_pair(pre):
    normal_cdf = 0.5 * (1.0 + lax.erf(pre * 0.7071067811865476))
    normal_pdf = jnp.exp(-0.5 * pre * pre) * 0.3989422804014327
    return pre * normal_cdf, normal_cdf + pre * normal_pdf


def kernel(
    tok_in, param_in, ograd_in, sout_in, x_in, win_in, wout_in,
    win_out, wout_out, tok, param_p, base, disp, back,
    param, ograd, sout, x, win, wout,
    xp, slope, act_t, grads, pgs, pg_t, sums,
    part, pair_part, lse_own, lse_pair,
    out_a, in_a, out_b, in_b,
    rs_out, rs_in, out_part,
    local_sem, pair_send, pair_recv, all_send, all_recv, all_self,
    ag_send, ag_recv, rs_send, rs_recv,
):
    width = tok.shape[1]
    cuts = width // LANES
    d = lax.axis_index("dp")
    e = lax.axis_index("expert")
    zh, y = d // RING, d % RING
    chip, core = e // 2, e % 2
    me = zh * CHIPS + chip
    other = (d, e + 1 - 2 * core)
    right = (zh * RING + (y + 1) % RING, e)
    left = (zh * RING + (y + RING - 1) % RING, e)

    z, line = zh * (CHIPS // ROW) + chip // ROW, chip % ROW
    length = BLOCK // ROW

    def peer(n):
        step = n // ROW
        far = (z + length // 2 + (step + 1) // 2 * (1 - 2 * (step % 2))) % length
        t = far * ROW + (line + n) % ROW
        return t, t % CHIPS, ((t // CHIPS) * RING + y, 2 * (t % CHIPS) + core)

    def for_peers(act):
        pl.loop(0, BLOCK - ROW)(act)
        pl.loop(BLOCK - ROW + 1, BLOCK)(act)

    loads = [
        pltpu.make_async_copy(src, dst, local_sem.at[i])
        for i, (src, dst) in enumerate(
            [(tok_in, tok), (param_in, param), (ograd_in, ograd), (x_in, x),
             (win_in, win), (sout_in, sout), (wout_in, wout)]
        )
    ]
    for load in loads[:3]:
        load.start()

    barrier = pltpu.get_barrier_semaphore()

    def greet(n):
        _, _, device = peer(n)
        pl.semaphore_signal(barrier, inc=1, device_id=device, device_id_type=MESH)

    for_peers(greet)
    for device in (other, left, right):
        pl.semaphore_signal(barrier, inc=1, device_id=device, device_id_type=MESH)

    def softmax(logits):
        ex = jnp.exp(logits - jnp.max(logits, axis=0, keepdims=True))
        return ex / jnp.sum(ex, axis=0, keepdims=True)

    loads[0].wait()
    loads[1].wait()
    combine = softmax(matmul_t(param[...], tok[...]))
    loads[2].wait()
    whole = matmul(combine.astype(BF16), ograd[...])
    for i in range(cuts):
        part[i] = whole[:, i * LANES:(i + 1) * LANES]
        out_part[i] = part[i, pl.ds(1 - core, CHIPS, stride=2), :]
    for load in loads[3:]:
        load.start()

    pl.semaphore_wait(barrier, BLOCK - 1 + 3)
    send_part = pltpu.make_async_remote_copy(
        out_part, pair_part, pair_send.at[0], pair_recv.at[0], device_id=other, device_id_type=MESH
    )
    send_part.start()
    send_part.wait_recv()
    slot_sum = [part[i, pl.ds(core, CHIPS, stride=2), :] + pair_part[i] for i in range(cuts)]
    for i in range(cuts // 2):
        out_a[:, i] = jnp.stack(slot_sum[2 * i:2 * i + 2], axis=1).astype(BF16)

    all_but_one = pl.ds(0, BLOCK - 1)

    def give_a(n):
        _, owner, device = peer(n)
        pltpu.make_async_remote_copy(
            out_a.at[owner], in_a.at[me], all_send.at[0], all_recv.at[0],
            device_id=device, device_id_type=MESH,
        ).start()

    for_peers(give_a)
    self_a = pltpu.make_async_copy(out_a.at[chip], in_a.at[me], all_self.at[0])
    self_a.start()

    mine = pl.ds(pl.multiple_of(CHIPS * core, 8), CHIPS)
    row = lax.broadcasted_iota(jnp.int32, (BLOCK, BLOCK), 0)
    col = lax.broadcasted_iota(jnp.int32, (BLOCK, BLOCK), 1)
    wanted = jnp.where(row < CHIPS, 2 * row, 2 * (row - CHIPS) + 1)
    perm = jnp.where(col == wanted, 1.0, 0.0).astype(BF16)
    param_p[...] = matmul(perm, param[...]).astype(BF16)
    logits = matmul_t(param_p[...], tok[...])
    combine = softmax(logits)
    col_max = jnp.max(logits, axis=1, keepdims=True)
    col_sum = jnp.sum(jnp.exp(logits - col_max), axis=1, keepdims=True)
    lse_own[...] = jnp.broadcast_to(col_max + jnp.log(col_sum), lse_own.shape)
    send_lse = pltpu.make_async_remote_copy(
        lse_own, lse_pair, pair_send.at[1], pair_recv.at[1], device_id=other, device_id_type=MESH
    )
    send_lse.start()
    loads[3].wait()
    for b in range(RING):
        lo = x[b * CHIPS:(b + 1) * CHIPS, :]
        hi = x[(RING + b) * CHIPS:(RING + b + 1) * CHIPS, :]
        xp[b * BLOCK:(b + 1) * BLOCK, :] = jnp.concatenate([lo, hi], axis=0)
    loads[4].wait()
    for i in range(xp.shape[0] // LANES):
        rows = slice(i * LANES, (i + 1) * LANES)
        act, rise = gelu_pair(matmul_t(xp[rows, :], win[...]))
        slope[rows, :] = rise
        act_t[:, rows] = act.T.astype(BF16)
    loads[5].wait()
    comb_grad = matmul_t(matmul(perm, sout[...]).astype(BF16), ograd[...])
    base[...] = combine * (comb_grad - jnp.sum(combine * comb_grad, axis=0, keepdims=True))
    send_lse.wait_recv()
    lse_a, lse_b = lse_own[...], lse_pair[...]
    top = jnp.maximum(lse_a, lse_b)
    lse = top + jnp.log(jnp.exp(lse_a - top) + jnp.exp(lse_b - top))
    disp[...] = jnp.exp(logits - lse)

    def rows_of(b):
        return pl.ds(pl.multiple_of(b * BLOCK, ALIGN), BLOCK)

    pltpu.make_async_copy(in_a.at[all_but_one], in_a.at[all_but_one], all_recv.at[0]).wait()
    self_a.wait()
    for i in range(cuts):
        grads[rows_of(y), i * LANES:(i + 1) * LANES] = in_a[:, i // 2].astype(F32)[:, i % 2].astype(BF16)
    loads[6].wait()

    def work(blocks):
        g = [grads[rows_of(b), :] for b in blocks]
        s = [slope[rows_of(b), :] for b in blocks]
        g = g[0] if len(g) == 1 else jnp.concatenate(g, axis=0)
        s = s[0] if len(s) == 1 else jnp.concatenate(s, axis=0)
        pg = (matmul_t(g, wout[...]) * s).astype(BF16)
        total = matmul(pg, win[...])
        for i, b in enumerate(blocks):
            pgs[rows_of(b), :] = pg[i * BLOCK:(i + 1) * BLOCK, :]
            sums[rows_of(b), :] = total[i * BLOCK:(i + 1) * BLOCK, :]

    def at(offset):
        return (y + offset + RING) % RING

    sides = (right, left)
    ag = {}
    for s in range(4):
        for i in range(2):
            rows = rows_of(at(-s if i == 0 else s))
            for c in OPPOSITE[i] if s == 3 else range(4):
                ref = grads.at[rows, pl.ds(*PARTS[c])]
                ag[s, i, c] = pltpu.make_async_remote_copy(
                    ref, ref, ag_send.at[s, i, c], ag_recv.at[s, i, c],
                    device_id=sides[i], device_id_type=MESH,
                )
    for c in range(4):
        for i in range(2):
            ag[0, i, c].start()
    work([at(0)])
    for s in range(1, 4):
        for c in (0, 2, 1, 3):
            for i in range(2):
                ag[s - 1, i, c].wait_recv()
                if (s, i, c) in ag:
                    ag[s, i, c].start()
        work([at(-s), at(s)])
    for i in range(2):
        for c in OPPOSITE[i]:
            ag[3, i, c].wait_recv()
    far = rows_of(at(4))
    far_grad = (matmul_t(grads[far, :], wout[...]) * slope[far, :]).astype(BF16)
    pgs[far, :] = far_grad

    chunk = 2 * LANES

    def weight_out():
        for i in range(width // chunk):
            lanes = slice(i * chunk, (i + 1) * chunk)
            wout_out[:, lanes] = matmul(act_t[...], grads[:, lanes]).astype(BF16)

    def transpose_pg():
        for i in range(pgs.shape[0] // LANES):
            rows = slice(i * LANES, (i + 1) * LANES)
            pg_t[:, rows] = pgs[rows, :].astype(F32).T.astype(BF16)

    def weight_in(first, last):
        for i in range(first, last):
            lanes = slice(i * chunk, (i + 1) * chunk)
            win_out[:, lanes] = matmul(pg_t[...], xp[:, lanes]).astype(BF16)

    rs = {}

    def give_sum(s, i, c):
        dest = rows_of(at(4 - s if i == 0 else s - 4))
        lanes = pl.ds(*PARTS[c])
        term = sums[dest, lanes] if s else matmul(far_grad, win[:, lanes])
        if (s - 1, i, c) in rs:
            rs[s - 1, i, c].wait_recv()
            term = term + rs_in[s - 1, i, :, lanes].astype(F32)
        rs_out[s, i, :, lanes] = term.astype(BF16)
        rs[s, i, c] = pltpu.make_async_remote_copy(
            rs_out.at[s, i, :, lanes], rs_in.at[s, i, :, lanes], rs_send.at[s, i, c], rs_recv.at[s, i, c],
            device_id=sides[i], device_id_type=MESH,
        )
        rs[s, i, c].start()

    def give_sums(s, late):
        for k in range(2):
            for i in range(2):
                give_sum(s, i, OPPOSITE[i if late else 1 - i][k])

    give_sums(0, True)
    give_sums(1, False)
    weight_out()
    transpose_pg()
    give_sums(1, True)
    give_sums(2, False)
    weight_in(0, 2)
    give_sums(2, True)
    give_sums(3, False)
    weight_in(2, 5)
    give_sums(3, True)
    for i in range(2):
        for c in range(4):
            rs[3, i, c].wait_recv()

    total = (sums[rows_of(y), :] + rs_in[3, 0].astype(F32) + rs_in[3, 1].astype(F32)).astype(BF16).astype(F32)
    dot = jnp.sum(xp[rows_of(y), :].astype(F32) * total, axis=1, keepdims=True)
    dot_hi = dot.astype(BF16).astype(F32)
    columns = [total[:, i * LANES:(i + 1) * LANES] for i in range(cuts)]
    columns += [jnp.broadcast_to(v, (BLOCK, LANES)) for v in (dot_hi, dot - dot_hi)]
    for i in range(cuts // 2 + 1):
        out_b[:, i] = jnp.stack(columns[2 * i:2 * i + 2], axis=1).astype(BF16)

    def give_b(n):
        t, _, device = peer(n)
        pltpu.make_async_remote_copy(
            out_b.at[t], in_b.at[me], all_send.at[1], all_recv.at[1],
            device_id=device, device_id_type=MESH,
        ).start()

    for_peers(give_b)
    self_b = pltpu.make_async_copy(out_b.at[me], in_b.at[me], all_self.at[1])
    self_b.start()
    pltpu.make_async_copy(in_b.at[all_but_one], in_b.at[all_but_one], all_recv.at[1]).wait()
    self_b.wait()

    for i in range(cuts // 2 + 1):
        v = in_b[:CHIPS, i].astype(F32) + in_b[CHIPS:, i].astype(F32)
        if i < cuts // 2:
            for k in range(2):
                back[mine, (2 * i + k) * LANES:(2 * i + k + 1) * LANES] = v[:, k]
        else:
            back[mine, width:width + LANES] = v[:, 0] + v[:, 1]
    send_back = pltpu.make_async_remote_copy(
        back.at[mine], back.at[mine], pair_send.at[2], pair_recv.at[2], device_id=other, device_id_type=MESH
    )
    send_back.start()
    send_back.wait_recv()

    send_part.wait_send()
    send_lse.wait_send()
    send_back.wait_send()
    for i, held in enumerate((in_a, in_b)):
        pltpu.make_async_copy(held.at[all_but_one], held.at[all_but_one], all_send.at[i]).wait()
    for copy in list(ag.values()) + list(rs.values()):
        copy.wait_send()


def finish(win_made, wout_made, tok, param_p, base, disp, back, tok_grad, win_grad, wout_grad, tok_out, sem):
    width = tok.shape[1]
    stores = [
        pltpu.make_async_copy(win_made, win_grad, sem.at[0]),
        pltpu.make_async_copy(wout_made, wout_grad, sem.at[1]),
    ]
    for store in stores:
        store.start()
    in_grad = back[:, :width].astype(BF16)
    disp_grad = matmul_t(in_grad, tok[...])
    logit_grad = base[...] + disp[...] * (disp_grad - back[:, width:width + LANES])
    left_t = jnp.concatenate([disp[...], logit_grad], axis=0).T.astype(BF16)
    half = width // 2
    for i in range(2):
        lanes = slice(i * half, (i + 1) * half)
        right_t = jnp.concatenate([in_grad[:, lanes], param_p[:, lanes]], axis=0)
        tok_out[:, lanes] = matmul(left_t, right_t).astype(BF16)
        store = pltpu.make_async_copy(tok_out.at[:, lanes], tok_grad.at[:, lanes], sem.at[2 + i])
        store.start()
        stores.append(store)
    for store in stores:
        store.wait()


def body(tokens, slot_param, out_grad, slot_outputs, slot_inputs, w_in, w_out):
    tok, ograd, sout = tokens[0], out_grad[0], slot_outputs[0]
    x = slot_inputs[:, 0]
    param = slot_param.T
    win, wout = w_in[0].T, w_out[0]
    images, width = x.shape
    hidden = wout.shape[0]
    slots = param.shape[0]
    tokens_here = tok.shape[0]
    pieces = width // (2 * LANES)
    vm = pltpu.VMEM
    dma = pltpu.SemaphoreType.DMA
    hbm = pl.BlockSpec(memory_space=pltpu.HBM)
    args = [pltpu.with_memory_space_constraint(v, pltpu.HBM) for v in (tok, param, ograd, sout, x, win, wout)]
    in_vmem = pl.BlockSpec(memory_space=pltpu.VMEM)
    made = pl.pallas_call(
        kernel,
        out_shape=(
            vm((hidden, width), BF16), vm((hidden, width), BF16), vm((tokens_here, width), BF16),
            vm((slots, width), BF16), vm((slots, LANES), F32), vm((slots, LANES), F32),
            vm((slots, width + LANES), F32),
        ),
        in_specs=[hbm] * 7,
        out_specs=(in_vmem,) * 7,
        scratch_shapes=[
            vm((slots, width), BF16), vm((tokens_here, width), BF16),
            vm((slots, width), BF16), vm((images, width), BF16), vm((hidden, width), BF16),
            vm((hidden, width), BF16),
            vm((images, width), BF16), vm((images, hidden), F32),
            vm((hidden, images), BF16), vm((images, width), BF16), vm((images, hidden), BF16),
            vm((hidden, images), BF16), vm((images, width), F32),
            vm((width // LANES, slots, LANES), F32), vm((width // LANES, CHIPS, LANES), F32),
            vm((slots, LANES), F32), vm((slots, LANES), F32),
            vm((CHIPS, pieces, 2, LANES), BF16), vm((BLOCK, pieces, 2, LANES), BF16),
            vm((BLOCK, pieces + 1, 2, LANES), BF16), vm((BLOCK, pieces + 1, 2, LANES), BF16),
            vm((4, 2, BLOCK, width), BF16), vm((4, 2, BLOCK, width), BF16),
            vm((width // LANES, CHIPS, LANES), F32),
            dma((7,)), dma((3,)), dma((3,)), dma((2,)), dma((2,)), dma((2,)),
            dma((4, 2, 4)), dma((4, 2, 4)), dma((4, 2, 4)), dma((4, 2, 4)),
        ],
        compiler_params=pltpu.CompilerParams(
            collective_id=0, has_side_effects=True, vmem_limit_bytes=40 * 1024 * 1024
        ),
    )(*args)
    tok_grad, win_grad, wout_grad = pl.pallas_call(
        finish,
        out_shape=(
            jax.ShapeDtypeStruct((tokens_here, width), BF16),
            jax.ShapeDtypeStruct((hidden, width), BF16),
            jax.ShapeDtypeStruct((hidden, width), BF16),
        ),
        in_specs=[in_vmem] * 7,
        out_specs=(hbm,) * 3,
        scratch_shapes=[vm((tokens_here, width), BF16), dma((4,))],
        compiler_params=pltpu.CompilerParams(vmem_limit_bytes=32 * 1024 * 1024),
    )(*made)
    return tok_grad[None], win_grad.T[None], wout_grad[None]


def solution(mesh):
    placed = (
        P(("dp", "expert"), None, None),
        P(),
        P(("dp", "expert"), None, None),
        P(("dp", "expert"), None, None),
        P(None, "expert", None),
        P("expert", None, "dp"),
        P("expert", "dp", None),
    )
    return jax.shard_map(
        body,
        mesh=mesh,
        in_specs=placed,
        out_specs=(
            P(("dp", "expert"), None, None),
            P("expert", None, "dp"),
            P("expert", "dp", None),
        ),
        check_vma=False,
    )
```

```python
import jax
import jax.numpy as jnp
from jax import lax
from jax.experimental import pallas as pl
from jax.experimental.pallas import tpu as pltpu
from jax.sharding import PartitionSpec as P

F32 = jnp.float32
BF16 = jnp.bfloat16
MESH = pl.DeviceIdType.MESH

RING = 8
HALVES = 2
ROW = 4
CHIPS = 24
BLOCK = HALVES * CHIPS
ALIGN = 16
LANES = 128
ROW_PARTS = BLOCK // ALIGN


def matmul(a, b):
    return lax.dot_general(a, b, (((1,), (0,)), ((), ())), preferred_element_type=F32)


def matmul_t(a, b):
    return lax.dot_general(a, b, (((1,), (1,)), ((), ())), preferred_element_type=F32)


def gelu_pair(pre):
    normal_cdf = 0.5 * (1.0 + lax.erf(pre * 0.7071067811865476))
    normal_pdf = jnp.exp(-0.5 * pre * pre) * 0.3989422804014327
    return pre * normal_cdf, normal_cdf + pre * normal_pdf


def kernel(
    tok_in, param_in, ograd_in, sout_in, x_in, win_in, wout_in,
    win_out, wout_out, tok, param_p, base, disp, back,
    param, ograd, sout, x, win, wout,
    xp, slope, act_t, grads, pgs, pg_t, sums,
    part, pair_part, lse_own, lse_pair,
    out_a, in_a, out_b, in_b,
    rs_out, rs_in, out_part,
    local_sem, pair_send, pair_recv, all_send, all_recv, all_self,
    ag_send, ag_recv, rs_send, rs_recv,
):
    width = tok.shape[1]
    cuts = width // LANES
    d = lax.axis_index("dp")
    e = lax.axis_index("expert")
    zh, y = d // RING, d % RING
    chip, core = e // 2, e % 2
    me = zh * CHIPS + chip
    other = (d, e + 1 - 2 * core)
    right = (zh * RING + (y + 1) % RING, e)
    left = (zh * RING + (y + RING - 1) % RING, e)

    z, line = zh * (CHIPS // ROW) + chip // ROW, chip % ROW
    length = BLOCK // ROW

    def peer(n):
        step = n // ROW
        far = (z + length // 2 + (step + 1) // 2 * (1 - 2 * (step % 2))) % length
        t = far * ROW + (line + n) % ROW
        return t, t % CHIPS, ((t // CHIPS) * RING + y, 2 * (t % CHIPS) + core)

    def for_peers(act):
        pl.loop(0, BLOCK - ROW)(act)
        pl.loop(BLOCK - ROW + 1, BLOCK)(act)

    loads = [
        pltpu.make_async_copy(src, dst, local_sem.at[i])
        for i, (src, dst) in enumerate(
            [(tok_in, tok), (param_in, param), (ograd_in, ograd), (x_in, x),
             (win_in, win), (sout_in, sout), (wout_in, wout)]
        )
    ]
    for load in loads[:3]:
        load.start()

    barrier = pltpu.get_barrier_semaphore()

    def greet(n):
        _, _, device = peer(n)
        pl.semaphore_signal(barrier, inc=1, device_id=device, device_id_type=MESH)

    for_peers(greet)
    for device in (other, left, right):
        pl.semaphore_signal(barrier, inc=1, device_id=device, device_id_type=MESH)

    def softmax(logits):
        ex = jnp.exp(logits - jnp.max(logits, axis=0, keepdims=True))
        return ex / jnp.sum(ex, axis=0, keepdims=True)

    loads[0].wait()
    loads[1].wait()
    combine = softmax(matmul_t(param[...], tok[...]))
    loads[2].wait()
    whole = matmul(combine.astype(BF16), ograd[...])
    for i in range(cuts):
        part[i] = whole[:, i * LANES:(i + 1) * LANES]
        out_part[i] = part[i, pl.ds(1 - core, CHIPS, stride=2), :]
    for load in loads[3:]:
        load.start()

    pl.semaphore_wait(barrier, BLOCK - 1 + 3)
    send_part = pltpu.make_async_remote_copy(
        out_part, pair_part, pair_send.at[0], pair_recv.at[0], device_id=other, device_id_type=MESH
    )
    send_part.start()
    send_part.wait_recv()
    slot_sum = [part[i, pl.ds(core, CHIPS, stride=2), :] + pair_part[i] for i in range(cuts)]
    for i in range(cuts // 2):
        out_a[:, i] = jnp.stack(slot_sum[2 * i:2 * i + 2], axis=1).astype(BF16)

    all_but_one = pl.ds(0, BLOCK - 1)

    def give_a(n):
        _, owner, device = peer(n)
        pltpu.make_async_remote_copy(
            out_a.at[owner], in_a.at[me], all_send.at[0], all_recv.at[0],
            device_id=device, device_id_type=MESH,
        ).start()

    for_peers(give_a)
    self_a = pltpu.make_async_copy(out_a.at[chip], in_a.at[me], all_self.at[0])
    self_a.start()

    mine = pl.ds(pl.multiple_of(CHIPS * core, 8), CHIPS)
    row = lax.broadcasted_iota(jnp.int32, (BLOCK, BLOCK), 0)
    col = lax.broadcasted_iota(jnp.int32, (BLOCK, BLOCK), 1)
    wanted = jnp.where(row < CHIPS, 2 * row, 2 * (row - CHIPS) + 1)
    perm = jnp.where(col == wanted, 1.0, 0.0).astype(BF16)
    param_p[...] = matmul(perm, param[...]).astype(BF16)
    logits = matmul_t(param_p[...], tok[...])
    combine = softmax(logits)
    col_max = jnp.max(logits, axis=1, keepdims=True)
    col_sum = jnp.sum(jnp.exp(logits - col_max), axis=1, keepdims=True)
    lse_own[...] = jnp.broadcast_to(col_max + jnp.log(col_sum), lse_own.shape)
    send_lse = pltpu.make_async_remote_copy(
        lse_own, lse_pair, pair_send.at[1], pair_recv.at[1], device_id=other, device_id_type=MESH
    )
    send_lse.start()
    loads[3].wait()
    for b in range(RING):
        lo = x[b * CHIPS:(b + 1) * CHIPS, :]
        hi = x[(RING + b) * CHIPS:(RING + b + 1) * CHIPS, :]
        xp[b * BLOCK:(b + 1) * BLOCK, :] = jnp.concatenate([lo, hi], axis=0)
    loads[4].wait()
    for i in range(xp.shape[0] // LANES):
        rows = slice(i * LANES, (i + 1) * LANES)
        act, rise = gelu_pair(matmul_t(xp[rows, :], win[...]))
        slope[rows, :] = rise
        act_t[:, rows] = act.T.astype(BF16)
    loads[5].wait()
    comb_grad = matmul_t(matmul(perm, sout[...]).astype(BF16), ograd[...])
    base[...] = combine * (comb_grad - jnp.sum(combine * comb_grad, axis=0, keepdims=True))
    send_lse.wait_recv()
    lse_a, lse_b = lse_own[...], lse_pair[...]
    top = jnp.maximum(lse_a, lse_b)
    lse = top + jnp.log(jnp.exp(lse_a - top) + jnp.exp(lse_b - top))
    disp[...] = jnp.exp(logits - lse)

    def rows_of(b):
        return pl.ds(pl.multiple_of(b * BLOCK, ALIGN), BLOCK)

    pltpu.make_async_copy(in_a.at[all_but_one], in_a.at[all_but_one], all_recv.at[0]).wait()
    self_a.wait()
    for i in range(cuts):
        grads[rows_of(y), i * LANES:(i + 1) * LANES] = in_a[:, i // 2].astype(F32)[:, i % 2].astype(BF16)
    loads[6].wait()

    def at(offset):
        return (y + offset + RING) % RING

    sides = (right, left)
    half = width // 2
    sides_lanes = (pl.ds(0, half), pl.ds(half, half))

    def rows_part(b, r):
        return pl.ds(pl.multiple_of(b * BLOCK + r * ALIGN, ALIGN), ALIGN)

    every = [(r, i if ahead else 1 - i, i) for ahead in (True, False) for r in range(ROW_PARTS) for i in range(2)]
    ag = {}
    for s in range(4):
        for r, h, i in every:
            if s < 3 or h == i:
                ref = grads.at[rows_part(at(-s if i == 0 else s), r), sides_lanes[h]]
                ag[s, r, h, i] = pltpu.make_async_remote_copy(
                    ref, ref, ag_send.at[s, i, r, h], ag_recv.at[s, i, r, h],
                    device_id=sides[i], device_id_type=MESH,
                )
    for r, h, i in every:
        ag[0, r, h, i].start()
    for s in range(1, 4):
        for r, h, i in every:
            ag[s - 1, r, h, i].wait_recv()
            if (s, r, h, i) in ag:
                ag[s, r, h, i].start()
    for r, h, i in every:
        if h == i:
            ag[3, r, h, i].wait_recv()

    far = rows_of(at(4))
    far_grad = (matmul_t(grads[far, :], wout[...]) * slope[far, :]).astype(BF16)
    rs = {}

    def give_sum(s, r, h, i, term):
        rows = pl.ds(r * ALIGN, ALIGN)
        rs_out[s, i, rows, sides_lanes[h]] = term.astype(BF16)
        rs[s, r, h, i] = pltpu.make_async_remote_copy(
            rs_out.at[s, i, rows, sides_lanes[h]], rs_in.at[s, i, rows, sides_lanes[h]],
            rs_send.at[s, i, r, h], rs_recv.at[s, i, r, h], device_id=sides[i], device_id_type=MESH,
        )
        rs[s, r, h, i].start()

    def give_sums(s, late):
        for r, h, i in every:
            if (h == i) == late:
                term = sums[rows_part(at(4 - s if i == 0 else s - 4), r), sides_lanes[h]]
                if (s - 1, r, h, i) in rs:
                    rs[s - 1, r, h, i].wait_recv()
                    term = term + rs_in[s - 1, i, r * ALIGN:(r + 1) * ALIGN, sides_lanes[h]].astype(F32)
                give_sum(s, r, h, i, term)

    for i in range(2):
        term = matmul(far_grad, win[:, sides_lanes[i]])
        for r in range(ROW_PARTS):
            give_sum(0, r, i, i, term[r * ALIGN:(r + 1) * ALIGN, :])

    pgs[...] = (matmul_t(grads[...], wout[...]) * slope[...]).astype(BF16)
    sums[...] = matmul(pgs[...], win[...])

    chunk = 2 * LANES

    def weight_out():
        for i in range(width // chunk):
            lanes = slice(i * chunk, (i + 1) * chunk)
            wout_out[:, lanes] = matmul(act_t[...], grads[:, lanes]).astype(BF16)

    def transpose_pg():
        for i in range(pgs.shape[0] // LANES):
            rows = slice(i * LANES, (i + 1) * LANES)
            pg_t[:, rows] = pgs[rows, :].astype(F32).T.astype(BF16)

    def weight_in():
        for i in range(width // chunk):
            lanes = slice(i * chunk, (i + 1) * chunk)
            win_out[:, lanes] = matmul(pg_t[...], xp[:, lanes]).astype(BF16)

    give_sums(1, False)
    weight_out()
    transpose_pg()
    give_sums(1, True)
    give_sums(2, False)
    give_sums(2, True)
    give_sums(3, False)
    give_sums(3, True)
    weight_in()
    for r, h, i in every:
        rs[3, r, h, i].wait_recv()

    total = (sums[rows_of(y), :] + rs_in[3, 0].astype(F32) + rs_in[3, 1].astype(F32)).astype(BF16).astype(F32)
    dot = jnp.sum(xp[rows_of(y), :].astype(F32) * total, axis=1, keepdims=True)
    dot_hi = dot.astype(BF16).astype(F32)
    columns = [total[:, i * LANES:(i + 1) * LANES] for i in range(cuts)]
    columns += [jnp.broadcast_to(v, (BLOCK, LANES)) for v in (dot_hi, dot - dot_hi)]
    for i in range(cuts // 2 + 1):
        out_b[:, i] = jnp.stack(columns[2 * i:2 * i + 2], axis=1).astype(BF16)

    def give_b(n):
        t, _, device = peer(n)
        pltpu.make_async_remote_copy(
            out_b.at[t], in_b.at[me], all_send.at[1], all_recv.at[1],
            device_id=device, device_id_type=MESH,
        ).start()

    for_peers(give_b)
    self_b = pltpu.make_async_copy(out_b.at[me], in_b.at[me], all_self.at[1])
    self_b.start()
    pltpu.make_async_copy(in_b.at[all_but_one], in_b.at[all_but_one], all_recv.at[1]).wait()
    self_b.wait()

    for i in range(cuts // 2 + 1):
        v = in_b[:CHIPS, i].astype(F32) + in_b[CHIPS:, i].astype(F32)
        if i < cuts // 2:
            for k in range(2):
                back[mine, (2 * i + k) * LANES:(2 * i + k + 1) * LANES] = v[:, k]
        else:
            back[mine, width:width + LANES] = v[:, 0] + v[:, 1]
    send_back = pltpu.make_async_remote_copy(
        back.at[mine], back.at[mine], pair_send.at[2], pair_recv.at[2], device_id=other, device_id_type=MESH
    )
    send_back.start()
    send_back.wait_recv()

    send_part.wait_send()
    send_lse.wait_send()
    send_back.wait_send()
    for i, held in enumerate((in_a, in_b)):
        pltpu.make_async_copy(held.at[all_but_one], held.at[all_but_one], all_send.at[i]).wait()
    for copy in list(ag.values()) + list(rs.values()):
        copy.wait_send()


def finish(win_made, wout_made, tok, param_p, base, disp, back, tok_grad, win_grad, wout_grad, tok_out, sem):
    width = tok.shape[1]
    stores = [
        pltpu.make_async_copy(win_made, win_grad, sem.at[0]),
        pltpu.make_async_copy(wout_made, wout_grad, sem.at[1]),
    ]
    for store in stores:
        store.start()
    in_grad = back[:, :width].astype(BF16)
    disp_grad = matmul_t(in_grad, tok[...])
    logit_grad = base[...] + disp[...] * (disp_grad - back[:, width:width + LANES])
    left_t = jnp.concatenate([disp[...], logit_grad], axis=0).T.astype(BF16)
    half = width // 2
    for i in range(2):
        lanes = slice(i * half, (i + 1) * half)
        right_t = jnp.concatenate([in_grad[:, lanes], param_p[:, lanes]], axis=0)
        tok_out[:, lanes] = matmul(left_t, right_t).astype(BF16)
        store = pltpu.make_async_copy(tok_out.at[:, lanes], tok_grad.at[:, lanes], sem.at[2 + i])
        store.start()
        stores.append(store)
    for store in stores:
        store.wait()


def body(tokens, slot_param, out_grad, slot_outputs, slot_inputs, w_in, w_out):
    tok, ograd, sout = tokens[0], out_grad[0], slot_outputs[0]
    x = slot_inputs[:, 0]
    param = slot_param.T
    win, wout = w_in[0].T, w_out[0]
    images, width = x.shape
    hidden = wout.shape[0]
    slots = param.shape[0]
    tokens_here = tok.shape[0]
    pieces = width // (2 * LANES)
    vm = pltpu.VMEM
    dma = pltpu.SemaphoreType.DMA
    hbm = pl.BlockSpec(memory_space=pltpu.HBM)
    args = [pltpu.with_memory_space_constraint(v, pltpu.HBM) for v in (tok, param, ograd, sout, x, win, wout)]
    in_vmem = pl.BlockSpec(memory_space=pltpu.VMEM)
    made = pl.pallas_call(
        kernel,
        out_shape=(
            vm((hidden, width), BF16), vm((hidden, width), BF16), vm((tokens_here, width), BF16),
            vm((slots, width), BF16), vm((slots, LANES), F32), vm((slots, LANES), F32),
            vm((slots, width + LANES), F32),
        ),
        in_specs=[hbm] * 7,
        out_specs=(in_vmem,) * 7,
        scratch_shapes=[
            vm((slots, width), BF16), vm((tokens_here, width), BF16),
            vm((slots, width), BF16), vm((images, width), BF16), vm((hidden, width), BF16),
            vm((hidden, width), BF16),
            vm((images, width), BF16), vm((images, hidden), F32),
            vm((hidden, images), BF16), vm((images, width), BF16), vm((images, hidden), BF16),
            vm((hidden, images), BF16), vm((images, width), F32),
            vm((width // LANES, slots, LANES), F32), vm((width // LANES, CHIPS, LANES), F32),
            vm((slots, LANES), F32), vm((slots, LANES), F32),
            vm((CHIPS, pieces, 2, LANES), BF16), vm((BLOCK, pieces, 2, LANES), BF16),
            vm((BLOCK, pieces + 1, 2, LANES), BF16), vm((BLOCK, pieces + 1, 2, LANES), BF16),
            vm((4, 2, BLOCK, width), BF16), vm((4, 2, BLOCK, width), BF16),
            vm((width // LANES, CHIPS, LANES), F32),
            dma((7,)), dma((3,)), dma((3,)), dma((2,)), dma((2,)), dma((2,)),
            dma((4, 2, ROW_PARTS, 2)), dma((4, 2, ROW_PARTS, 2)), dma((4, 2, ROW_PARTS, 2)),
            dma((4, 2, ROW_PARTS, 2)),
        ],
        compiler_params=pltpu.CompilerParams(
            collective_id=0, has_side_effects=True, vmem_limit_bytes=40 * 1024 * 1024
        ),
    )(*args)
    tok_grad, win_grad, wout_grad = pl.pallas_call(
        finish,
        out_shape=(
            jax.ShapeDtypeStruct((tokens_here, width), BF16),
            jax.ShapeDtypeStruct((hidden, width), BF16),
            jax.ShapeDtypeStruct((hidden, width), BF16),
        ),
        in_specs=[in_vmem] * 7,
        out_specs=(hbm,) * 3,
        scratch_shapes=[vm((tokens_here, width), BF16), dma((4,))],
        compiler_params=pltpu.CompilerParams(vmem_limit_bytes=32 * 1024 * 1024),
    )(*made)
    return tok_grad[None], win_grad.T[None], wout_grad[None]


def solution(mesh):
    placed = (
        P(("dp", "expert"), None, None),
        P(),
        P(("dp", "expert"), None, None),
        P(("dp", "expert"), None, None),
        P(None, "expert", None),
        P("expert", None, "dp"),
        P("expert", "dp", None),
    )
    return jax.shard_map(
        body,
        mesh=mesh,
        in_specs=placed,
        out_specs=(
            P(("dp", "expert"), None, None),
            P("expert", None, "dp"),
            P("expert", "dp", None),
        ),
        check_vma=False,
    )
```

```python
import jax
import jax.numpy as jnp
from jax import lax
from jax.experimental import pallas as pl
from jax.experimental.pallas import tpu as pltpu
from jax.sharding import PartitionSpec as P

F32 = jnp.float32
BF16 = jnp.bfloat16
MESH = pl.DeviceIdType.MESH

RING = 8
HALVES = 2
ROW = 4
CHIPS = 24
BLOCK = HALVES * CHIPS
ALIGN = 16
LANES = 128
ROW_PARTS = BLOCK // ALIGN


def matmul(a, b):
    return lax.dot_general(a, b, (((1,), (0,)), ((), ())), preferred_element_type=F32)


def matmul_t(a, b):
    return lax.dot_general(a, b, (((1,), (1,)), ((), ())), preferred_element_type=F32)


def gelu_pair(pre):
    normal_cdf = 0.5 * (1.0 + lax.erf(pre * 0.7071067811865476))
    normal_pdf = jnp.exp(-0.5 * pre * pre) * 0.3989422804014327
    return pre * normal_cdf, normal_cdf + pre * normal_pdf


def kernel(
    tok_in, param_in, ograd_in, sout_in, x_in, win_in, wout_in,
    win_out, wout_out, tok, param_p, base, disp, back,
    param, ograd, sout, x, win, wout,
    xp, slope, act_t, grads, pgs, pg_t, sums,
    part, pair_part, lse_own, lse_pair,
    out_a, in_a, out_b, in_b,
    rs_out, rs_in, out_part,
    local_sem, pair_send, pair_recv, all_send, all_recv, all_self,
    ag_send, ag_recv, rs_send, rs_recv,
):
    width = tok.shape[1]
    cuts = width // LANES
    d = lax.axis_index("dp")
    e = lax.axis_index("expert")
    zh, y = d // RING, d % RING
    chip, core = e // 2, e % 2
    me = zh * CHIPS + chip
    other = (d, e + 1 - 2 * core)
    right = (zh * RING + (y + 1) % RING, e)
    left = (zh * RING + (y + RING - 1) % RING, e)
    right2 = (zh * RING + (y + 2) % RING, e)
    left2 = (zh * RING + (y + RING - 2) % RING, e)

    z, line = zh * (CHIPS // ROW) + chip // ROW, chip % ROW
    length = BLOCK // ROW

    def peer(n):
        step = n // ROW
        far = (z + length // 2 + (step + 1) // 2 * (1 - 2 * (step % 2))) % length
        t = far * ROW + (line + n) % ROW
        return t, t % CHIPS, ((t // CHIPS) * RING + y, 2 * (t % CHIPS) + core)

    def for_peers(act):
        pl.loop(0, BLOCK - ROW)(act)
        pl.loop(BLOCK - ROW + 1, BLOCK)(act)

    loads = [
        pltpu.make_async_copy(src, dst, local_sem.at[i])
        for i, (src, dst) in enumerate(
            [(tok_in, tok), (param_in, param), (ograd_in, ograd), (x_in, x),
             (win_in, win), (sout_in, sout), (wout_in, wout)]
        )
    ]
    for load in loads[:3]:
        load.start()

    barrier = pltpu.get_barrier_semaphore()

    def greet(n):
        _, _, device = peer(n)
        pl.semaphore_signal(barrier, inc=1, device_id=device, device_id_type=MESH)

    for_peers(greet)
    for device in (other, left, right, left2, right2):
        pl.semaphore_signal(barrier, inc=1, device_id=device, device_id_type=MESH)

    def softmax(logits):
        ex = jnp.exp(logits - jnp.max(logits, axis=0, keepdims=True))
        return ex / jnp.sum(ex, axis=0, keepdims=True)

    loads[0].wait()
    loads[1].wait()
    combine = softmax(matmul_t(param[...], tok[...]))
    loads[2].wait()
    whole = matmul(combine.astype(BF16), ograd[...])
    for i in range(cuts):
        part[i] = whole[:, i * LANES:(i + 1) * LANES]
        out_part[i] = part[i, pl.ds(1 - core, CHIPS, stride=2), :]
    for load in loads[3:]:
        load.start()

    pl.semaphore_wait(barrier, BLOCK - 1 + 5)
    send_part = pltpu.make_async_remote_copy(
        out_part, pair_part, pair_send.at[0], pair_recv.at[0], device_id=other, device_id_type=MESH
    )
    send_part.start()
    send_part.wait_recv()
    slot_sum = [part[i, pl.ds(core, CHIPS, stride=2), :] + pair_part[i] for i in range(cuts)]
    for i in range(cuts // 2):
        out_a[:, i] = jnp.stack(slot_sum[2 * i:2 * i + 2], axis=1).astype(BF16)

    all_but_one = pl.ds(0, BLOCK - 1)

    def give_a(n):
        _, owner, device = peer(n)
        pltpu.make_async_remote_copy(
            out_a.at[owner], in_a.at[me], all_send.at[0], all_recv.at[0],
            device_id=device, device_id_type=MESH,
        ).start()

    for_peers(give_a)
    self_a = pltpu.make_async_copy(out_a.at[chip], in_a.at[me], all_self.at[0])
    self_a.start()

    mine = pl.ds(pl.multiple_of(CHIPS * core, 8), CHIPS)
    row = lax.broadcasted_iota(jnp.int32, (BLOCK, BLOCK), 0)
    col = lax.broadcasted_iota(jnp.int32, (BLOCK, BLOCK), 1)
    wanted = jnp.where(row < CHIPS, 2 * row, 2 * (row - CHIPS) + 1)
    perm = jnp.where(col == wanted, 1.0, 0.0).astype(BF16)
    param_p[...] = matmul(perm, param[...]).astype(BF16)
    logits = matmul_t(param_p[...], tok[...])
    combine = softmax(logits)
    col_max = jnp.max(logits, axis=1, keepdims=True)
    col_sum = jnp.sum(jnp.exp(logits - col_max), axis=1, keepdims=True)
    lse_own[...] = jnp.broadcast_to(col_max + jnp.log(col_sum), lse_own.shape)
    send_lse = pltpu.make_async_remote_copy(
        lse_own, lse_pair, pair_send.at[1], pair_recv.at[1], device_id=other, device_id_type=MESH
    )
    send_lse.start()
    loads[3].wait()
    for b in range(RING):
        lo = x[b * CHIPS:(b + 1) * CHIPS, :]
        hi = x[(RING + b) * CHIPS:(RING + b + 1) * CHIPS, :]
        xp[b * BLOCK:(b + 1) * BLOCK, :] = jnp.concatenate([lo, hi], axis=0)
    loads[4].wait()
    for i in range(xp.shape[0] // LANES):
        rows = slice(i * LANES, (i + 1) * LANES)
        act, rise = gelu_pair(matmul_t(xp[rows, :], win[...]))
        slope[rows, :] = rise
        act_t[:, rows] = act.T.astype(BF16)
    loads[5].wait()
    comb_grad = matmul_t(matmul(perm, sout[...]).astype(BF16), ograd[...])
    base[...] = combine * (comb_grad - jnp.sum(combine * comb_grad, axis=0, keepdims=True))
    send_lse.wait_recv()
    lse_a, lse_b = lse_own[...], lse_pair[...]
    top = jnp.maximum(lse_a, lse_b)
    lse = top + jnp.log(jnp.exp(lse_a - top) + jnp.exp(lse_b - top))
    disp[...] = jnp.exp(logits - lse)

    def rows_of(b):
        return pl.ds(pl.multiple_of(b * BLOCK, ALIGN), BLOCK)

    pltpu.make_async_copy(in_a.at[all_but_one], in_a.at[all_but_one], all_recv.at[0]).wait()
    self_a.wait()
    for i in range(cuts):
        grads[rows_of(y), i * LANES:(i + 1) * LANES] = in_a[:, i // 2].astype(F32)[:, i % 2].astype(BF16)
    loads[6].wait()

    def at(offset):
        return (y + offset + RING) % RING

    sides, skips = (right, left), (right2, left2)
    half = width // 2
    sides_lanes = (pl.ds(0, half), pl.ds(half, half))

    def rows_part(b, r):
        return pl.ds(pl.multiple_of(b * BLOCK + r * ALIGN, ALIGN), ALIGN)

    every = [(r, i if ahead else 1 - i, i) for ahead in (True, False) for r in range(ROW_PARTS) for i in range(2)]
    ag = {}
    for s in range(4):
        for r, h, i in every:
            if s < 3 or h == i:
                away = min(s, 2)
                ref = grads.at[rows_part(at(-away if i == 0 else away), r), sides_lanes[h]]
                ag[s, r, h, i] = pltpu.make_async_remote_copy(
                    ref, ref, ag_send.at[s, i, r, h], ag_recv.at[s, i, r, h],
                    device_id=(skips if s == 3 else sides)[i], device_id_type=MESH,
                )
    for r, h, i in every:
        ag[0, r, h, i].start()
    for s in range(1, 3):
        for r, h, i in every:
            ag[s - 1, r, h, i].wait_recv()
            if s == 2 and h == i:
                ag[3, r, h, i].start()
            ag[s, r, h, i].start()
    for s in range(2, 4):
        for r, h, i in every:
            if s == 2 or h == i:
                ag[s, r, h, i].wait_recv()

    far = rows_of(at(4))
    far_grad = (matmul_t(grads[far, :], wout[...]) * slope[far, :]).astype(BF16)
    rs = {}

    def give_sum(s, r, h, i, term):
        rows = pl.ds(r * ALIGN, ALIGN)
        rs_out[s, i, rows, sides_lanes[h]] = term.astype(BF16)
        rs[s, r, h, i] = pltpu.make_async_remote_copy(
            rs_out.at[s, i, rows, sides_lanes[h]], rs_in.at[s, i, rows, sides_lanes[h]],
            rs_send.at[s, i, r, h], rs_recv.at[s, i, r, h], device_id=sides[i], device_id_type=MESH,
        )
        rs[s, r, h, i].start()

    def give_sums(s, late):
        for r, h, i in every:
            if (h == i) == late:
                term = sums[rows_part(at(4 - s if i == 0 else s - 4), r), sides_lanes[h]]
                if (s - 1, r, h, i) in rs:
                    rs[s - 1, r, h, i].wait_recv()
                    term = term + rs_in[s - 1, i, r * ALIGN:(r + 1) * ALIGN, sides_lanes[h]].astype(F32)
                give_sum(s, r, h, i, term)

    for i in range(2):
        term = matmul(far_grad, win[:, sides_lanes[i]])
        for r in range(ROW_PARTS):
            give_sum(0, r, i, i, term[r * ALIGN:(r + 1) * ALIGN, :])

    pgs[...] = (matmul_t(grads[...], wout[...]) * slope[...]).astype(BF16)
    sums[...] = matmul(pgs[...], win[...])

    chunk = 2 * LANES

    def weight_out():
        for i in range(width // chunk):
            lanes = slice(i * chunk, (i + 1) * chunk)
            wout_out[:, lanes] = matmul(act_t[...], grads[:, lanes]).astype(BF16)

    def transpose_pg():
        for i in range(pgs.shape[0] // LANES):
            rows = slice(i * LANES, (i + 1) * LANES)
            pg_t[:, rows] = pgs[rows, :].astype(F32).T.astype(BF16)

    def weight_in():
        for i in range(width // chunk):
            lanes = slice(i * chunk, (i + 1) * chunk)
            win_out[:, lanes] = matmul(pg_t[...], xp[:, lanes]).astype(BF16)

    give_sums(1, False)
    weight_out()
    transpose_pg()
    give_sums(1, True)
    give_sums(2, False)
    give_sums(2, True)
    give_sums(3, False)
    give_sums(3, True)
    weight_in()
    for r, h, i in every:
        rs[3, r, h, i].wait_recv()

    total = (sums[rows_of(y), :] + rs_in[3, 0].astype(F32) + rs_in[3, 1].astype(F32)).astype(BF16).astype(F32)
    dot = jnp.sum(xp[rows_of(y), :].astype(F32) * total, axis=1, keepdims=True)
    dot_hi = dot.astype(BF16).astype(F32)
    columns = [total[:, i * LANES:(i + 1) * LANES] for i in range(cuts)]
    columns += [jnp.broadcast_to(v, (BLOCK, LANES)) for v in (dot_hi, dot - dot_hi)]
    for i in range(cuts // 2 + 1):
        out_b[:, i] = jnp.stack(columns[2 * i:2 * i + 2], axis=1).astype(BF16)

    def give_b(n):
        t, _, device = peer(n)
        pltpu.make_async_remote_copy(
            out_b.at[t], in_b.at[me], all_send.at[1], all_recv.at[1],
            device_id=device, device_id_type=MESH,
        ).start()

    for_peers(give_b)
    self_b = pltpu.make_async_copy(out_b.at[me], in_b.at[me], all_self.at[1])
    self_b.start()
    pltpu.make_async_copy(in_b.at[all_but_one], in_b.at[all_but_one], all_recv.at[1]).wait()
    self_b.wait()

    for i in range(cuts // 2 + 1):
        v = in_b[:CHIPS, i].astype(F32) + in_b[CHIPS:, i].astype(F32)
        if i < cuts // 2:
            for k in range(2):
                back[mine, (2 * i + k) * LANES:(2 * i + k + 1) * LANES] = v[:, k]
        else:
            back[mine, width:width + LANES] = v[:, 0] + v[:, 1]
    send_back = pltpu.make_async_remote_copy(
        back.at[mine], back.at[mine], pair_send.at[2], pair_recv.at[2], device_id=other, device_id_type=MESH
    )
    send_back.start()
    send_back.wait_recv()

    send_part.wait_send()
    send_lse.wait_send()
    send_back.wait_send()
    for i, held in enumerate((in_a, in_b)):
        pltpu.make_async_copy(held.at[all_but_one], held.at[all_but_one], all_send.at[i]).wait()
    for copy in list(ag.values()) + list(rs.values()):
        copy.wait_send()


def finish(win_made, wout_made, tok, param_p, base, disp, back, tok_grad, win_grad, wout_grad, tok_out, sem):
    width = tok.shape[1]
    stores = [
        pltpu.make_async_copy(win_made, win_grad, sem.at[0]),
        pltpu.make_async_copy(wout_made, wout_grad, sem.at[1]),
    ]
    for store in stores:
        store.start()
    in_grad = back[:, :width].astype(BF16)
    disp_grad = matmul_t(in_grad, tok[...])
    logit_grad = base[...] + disp[...] * (disp_grad - back[:, width:width + LANES])
    left_t = jnp.concatenate([disp[...], logit_grad], axis=0).T.astype(BF16)
    half = width // 2
    for i in range(2):
        lanes = slice(i * half, (i + 1) * half)
        right_t = jnp.concatenate([in_grad[:, lanes], param_p[:, lanes]], axis=0)
        tok_out[:, lanes] = matmul(left_t, right_t).astype(BF16)
        store = pltpu.make_async_copy(tok_out.at[:, lanes], tok_grad.at[:, lanes], sem.at[2 + i])
        store.start()
        stores.append(store)
    for store in stores:
        store.wait()


def body(tokens, slot_param, out_grad, slot_outputs, slot_inputs, w_in, w_out):
    tok, ograd, sout = tokens[0], out_grad[0], slot_outputs[0]
    x = slot_inputs[:, 0]
    param = slot_param.T
    win, wout = w_in[0].T, w_out[0]
    images, width = x.shape
    hidden = wout.shape[0]
    slots = param.shape[0]
    tokens_here = tok.shape[0]
    pieces = width // (2 * LANES)
    vm = pltpu.VMEM
    dma = pltpu.SemaphoreType.DMA
    hbm = pl.BlockSpec(memory_space=pltpu.HBM)
    args = [pltpu.with_memory_space_constraint(v, pltpu.HBM) for v in (tok, param, ograd, sout, x, win, wout)]
    in_vmem = pl.BlockSpec(memory_space=pltpu.VMEM)
    made = pl.pallas_call(
        kernel,
        out_shape=(
            vm((hidden, width), BF16), vm((hidden, width), BF16), vm((tokens_here, width), BF16),
            vm((slots, width), BF16), vm((slots, LANES), F32), vm((slots, LANES), F32),
            vm((slots, width + LANES), F32),
        ),
        in_specs=[hbm] * 7,
        out_specs=(in_vmem,) * 7,
        scratch_shapes=[
            vm((slots, width), BF16), vm((tokens_here, width), BF16),
            vm((slots, width), BF16), vm((images, width), BF16), vm((hidden, width), BF16),
            vm((hidden, width), BF16),
            vm((images, width), BF16), vm((images, hidden), F32),
            vm((hidden, images), BF16), vm((images, width), BF16), vm((images, hidden), BF16),
            vm((hidden, images), BF16), vm((images, width), F32),
            vm((width // LANES, slots, LANES), F32), vm((width // LANES, CHIPS, LANES), F32),
            vm((slots, LANES), F32), vm((slots, LANES), F32),
            vm((CHIPS, pieces, 2, LANES), BF16), vm((BLOCK, pieces, 2, LANES), BF16),
            vm((BLOCK, pieces + 1, 2, LANES), BF16), vm((BLOCK, pieces + 1, 2, LANES), BF16),
            vm((4, 2, BLOCK, width), BF16), vm((4, 2, BLOCK, width), BF16),
            vm((width // LANES, CHIPS, LANES), F32),
            dma((7,)), dma((3,)), dma((3,)), dma((2,)), dma((2,)), dma((2,)),
            dma((4, 2, ROW_PARTS, 2)), dma((4, 2, ROW_PARTS, 2)), dma((4, 2, ROW_PARTS, 2)),
            dma((4, 2, ROW_PARTS, 2)),
        ],
        compiler_params=pltpu.CompilerParams(
            collective_id=0, has_side_effects=True, vmem_limit_bytes=40 * 1024 * 1024
        ),
    )(*args)
    tok_grad, win_grad, wout_grad = pl.pallas_call(
        finish,
        out_shape=(
            jax.ShapeDtypeStruct((tokens_here, width), BF16),
            jax.ShapeDtypeStruct((hidden, width), BF16),
            jax.ShapeDtypeStruct((hidden, width), BF16),
        ),
        in_specs=[in_vmem] * 7,
        out_specs=(hbm,) * 3,
        scratch_shapes=[vm((tokens_here, width), BF16), dma((4,))],
        compiler_params=pltpu.CompilerParams(vmem_limit_bytes=32 * 1024 * 1024),
    )(*made)
    return tok_grad[None], win_grad.T[None], wout_grad[None]


def solution(mesh):
    placed = (
        P(("dp", "expert"), None, None),
        P(),
        P(("dp", "expert"), None, None),
        P(("dp", "expert"), None, None),
        P(None, "expert", None),
        P("expert", None, "dp"),
        P("expert", "dp", None),
    )
    return jax.shard_map(
        body,
        mesh=mesh,
        in_specs=placed,
        out_specs=(
            P(("dp", "expert"), None, None),
            P("expert", None, "dp"),
            P("expert", "dp", None),
        ),
        check_vma=False,
    )
```

```python
import jax
import jax.numpy as jnp
from jax import lax
from jax.experimental import pallas as pl
from jax.experimental.pallas import tpu as pltpu
from jax.sharding import PartitionSpec as P

F32 = jnp.float32
BF16 = jnp.bfloat16
MESH = pl.DeviceIdType.MESH

RING = 8
HALVES = 2
ROW = 4
CHIPS = 24
BLOCK = HALVES * CHIPS
ALIGN = 16
LANES = 128
ROW_PARTS = BLOCK // ALIGN


def matmul(a, b):
    return lax.dot_general(a, b, (((1,), (0,)), ((), ())), preferred_element_type=F32)


def matmul_t(a, b):
    return lax.dot_general(a, b, (((1,), (1,)), ((), ())), preferred_element_type=F32)


def gelu_pair(pre):
    normal_cdf = 0.5 * (1.0 + lax.erf(pre * 0.7071067811865476))
    normal_pdf = jnp.exp(-0.5 * pre * pre) * 0.3989422804014327
    return pre * normal_cdf, normal_cdf + pre * normal_pdf


def kernel(
    tok_in, param_in, ograd_in, sout_in, x_in, win_in, wout_in,
    win_out, wout_out, tok, param_p, base, disp, back,
    param, ograd, sout, x, win, wout,
    xp, slope, act_t, grads, pgs, pg_t, sums,
    part, pair_part, lse_own, lse_pair,
    out_a, in_a, out_b, in_b,
    rs_out, rs_in, out_part,
    local_sem, pair_send, pair_recv, all_send, all_recv, all_self,
    ag_send, ag_recv, rs_send, rs_recv,
):
    width = tok.shape[1]
    cuts = width // LANES
    d = lax.axis_index("dp")
    e = lax.axis_index("expert")
    zh, y = d // RING, d % RING
    chip, core = e // 2, e % 2
    me = zh * CHIPS + chip
    other = (d, e + 1 - 2 * core)
    right = (zh * RING + (y + 1) % RING, e)
    left = (zh * RING + (y + RING - 1) % RING, e)
    right2 = (zh * RING + (y + 2) % RING, e)
    left2 = (zh * RING + (y + RING - 2) % RING, e)

    z, line = zh * (CHIPS // ROW) + chip // ROW, chip % ROW
    length = BLOCK // ROW

    def peer(n):
        step = n // ROW
        far = (z + length // 2 + (step + 1) // 2 * (1 - 2 * (step % 2))) % length
        t = far * ROW + (line + n) % ROW
        return t, t % CHIPS, ((t // CHIPS) * RING + y, 2 * (t % CHIPS) + core)

    def for_peers(act):
        pl.loop(0, BLOCK - ROW)(act)
        pl.loop(BLOCK - ROW + 1, BLOCK)(act)

    loads = [
        pltpu.make_async_copy(src, dst, local_sem.at[i])
        for i, (src, dst) in enumerate(
            [(tok_in, tok), (param_in, param), (ograd_in, ograd), (x_in, x),
             (win_in, win), (sout_in, sout), (wout_in, wout)]
        )
    ]
    for load in loads[:3]:
        load.start()

    barrier = pltpu.get_barrier_semaphore()

    def greet(n):
        _, _, device = peer(n)
        pl.semaphore_signal(barrier, inc=1, device_id=device, device_id_type=MESH)

    for_peers(greet)
    for device in (other, left, right, left2, right2):
        pl.semaphore_signal(barrier, inc=1, device_id=device, device_id_type=MESH)

    def softmax(logits):
        ex = jnp.exp(logits - jnp.max(logits, axis=0, keepdims=True))
        return ex / jnp.sum(ex, axis=0, keepdims=True)

    loads[0].wait()
    loads[1].wait()
    combine = softmax(matmul_t(param[...], tok[...]))
    loads[2].wait()
    whole = matmul(combine.astype(BF16), ograd[...])
    for i in range(cuts):
        part[i] = whole[:, i * LANES:(i + 1) * LANES]
        out_part[i] = part[i, pl.ds(1 - core, CHIPS, stride=2), :]
    for load in loads[3:]:
        load.start()

    pl.semaphore_wait(barrier, BLOCK - 1 + 5)
    send_part = pltpu.make_async_remote_copy(
        out_part, pair_part, pair_send.at[0], pair_recv.at[0], device_id=other, device_id_type=MESH
    )
    send_part.start()
    send_part.wait_recv()
    slot_sum = [part[i, pl.ds(core, CHIPS, stride=2), :] + pair_part[i] for i in range(cuts)]
    for i in range(cuts // 2):
        out_a[:, i] = jnp.stack(slot_sum[2 * i:2 * i + 2], axis=1).astype(BF16)

    all_but_one = pl.ds(0, BLOCK - 1)

    def give_a(n):
        _, owner, device = peer(n)
        pltpu.make_async_remote_copy(
            out_a.at[owner], in_a.at[me], all_send.at[0], all_recv.at[0],
            device_id=device, device_id_type=MESH,
        ).start()

    for_peers(give_a)
    self_a = pltpu.make_async_copy(out_a.at[chip], in_a.at[me], all_self.at[0])
    self_a.start()

    mine = pl.ds(pl.multiple_of(CHIPS * core, 8), CHIPS)
    row = lax.broadcasted_iota(jnp.int32, (BLOCK, BLOCK), 0)
    col = lax.broadcasted_iota(jnp.int32, (BLOCK, BLOCK), 1)
    wanted = jnp.where(row < CHIPS, 2 * row, 2 * (row - CHIPS) + 1)
    perm = jnp.where(col == wanted, 1.0, 0.0).astype(BF16)
    param_p[...] = matmul(perm, param[...]).astype(BF16)
    logits = matmul_t(param_p[...], tok[...])
    combine = softmax(logits)
    col_max = jnp.max(logits, axis=1, keepdims=True)
    col_sum = jnp.sum(jnp.exp(logits - col_max), axis=1, keepdims=True)
    lse_own[...] = jnp.broadcast_to(col_max + jnp.log(col_sum), lse_own.shape)
    send_lse = pltpu.make_async_remote_copy(
        lse_own, lse_pair, pair_send.at[1], pair_recv.at[1], device_id=other, device_id_type=MESH
    )
    send_lse.start()
    loads[3].wait()
    for b in range(RING):
        lo = x[b * CHIPS:(b + 1) * CHIPS, :]
        hi = x[(RING + b) * CHIPS:(RING + b + 1) * CHIPS, :]
        xp[b * BLOCK:(b + 1) * BLOCK, :] = jnp.concatenate([lo, hi], axis=0)
    loads[4].wait()
    for i in range(xp.shape[0] // LANES):
        rows = slice(i * LANES, (i + 1) * LANES)
        act, rise = gelu_pair(matmul_t(xp[rows, :], win[...]))
        slope[rows, :] = rise
        act_t[:, rows] = act.T.astype(BF16)
    loads[5].wait()
    comb_grad = matmul_t(matmul(perm, sout[...]).astype(BF16), ograd[...])
    base[...] = combine * (comb_grad - jnp.sum(combine * comb_grad, axis=0, keepdims=True))
    send_lse.wait_recv()
    lse_a, lse_b = lse_own[...], lse_pair[...]
    top = jnp.maximum(lse_a, lse_b)
    lse = top + jnp.log(jnp.exp(lse_a - top) + jnp.exp(lse_b - top))
    disp[...] = jnp.exp(logits - lse)

    def rows_of(b):
        return pl.ds(pl.multiple_of(b * BLOCK, ALIGN), BLOCK)

    pltpu.make_async_copy(in_a.at[all_but_one], in_a.at[all_but_one], all_recv.at[0]).wait()
    self_a.wait()
    for i in range(cuts):
        grads[rows_of(y), i * LANES:(i + 1) * LANES] = in_a[:, i // 2].astype(F32)[:, i % 2].astype(BF16)
    loads[6].wait()

    def at(offset):
        return (y + offset + RING) % RING

    sides, skips = (right, left), (right2, left2)
    half = width // 2
    sides_lanes = (pl.ds(0, half), pl.ds(half, half))

    def place(r):
        return zh * r + (1 - zh) * (ROW_PARTS - 1 - r)

    def rows_part(b, r):
        return pl.ds(pl.multiple_of(b * BLOCK + place(r) * ALIGN, ALIGN), ALIGN)

    every = [(r, i if ahead else 1 - i, i) for ahead in (True, False) for r in range(ROW_PARTS) for i in range(2)]
    ag = {}
    for s in range(4):
        for r, h, i in every:
            if s < 3 or h == i:
                away = min(s, 2)
                ref = grads.at[rows_part(at(-away if i == 0 else away), r), sides_lanes[h]]
                ag[s, r, h, i] = pltpu.make_async_remote_copy(
                    ref, ref, ag_send.at[s, i, r, h], ag_recv.at[s, i, r, h],
                    device_id=(skips if s == 3 else sides)[i], device_id_type=MESH,
                )
    for r, h, i in every:
        ag[0, r, h, i].start()
    for s in range(1, 3):
        for r, h, i in every:
            ag[s - 1, r, h, i].wait_recv()
            if s == 2 and h == i:
                ag[3, r, h, i].start()
            ag[s, r, h, i].start()
    for s in range(2, 4):
        for r, h, i in every:
            if s == 2 or h == i:
                ag[s, r, h, i].wait_recv()

    far = rows_of(at(4))
    far_grad = (matmul_t(grads[far, :], wout[...]) * slope[far, :]).astype(BF16)
    rs = {}

    def give_sum(s, r, h, i, term):
        rows = pl.ds(r * ALIGN, ALIGN)
        rs_out[s, i, rows, sides_lanes[h]] = term.astype(BF16)
        rs[s, r, h, i] = pltpu.make_async_remote_copy(
            rs_out.at[s, i, rows, sides_lanes[h]], rs_in.at[s, i, rows, sides_lanes[h]],
            rs_send.at[s, i, r, h], rs_recv.at[s, i, r, h], device_id=sides[i], device_id_type=MESH,
        )
        rs[s, r, h, i].start()

    def give_sums(s, late):
        for r, h, i in every:
            if (h == i) == late:
                term = sums[rows_part(at(4 - s if i == 0 else s - 4), r), sides_lanes[h]]
                if (s - 1, r, h, i) in rs:
                    rs[s - 1, r, h, i].wait_recv()
                    term = term + rs_in[s - 1, i, r * ALIGN:(r + 1) * ALIGN, sides_lanes[h]].astype(F32)
                give_sum(s, r, h, i, term)

    for i in range(2):
        sums[far, sides_lanes[i]] = matmul(far_grad, win[:, sides_lanes[i]])
        for r in range(ROW_PARTS):
            give_sum(0, r, i, i, sums[rows_part(at(4), r), sides_lanes[i]])

    pgs[...] = (matmul_t(grads[...], wout[...]) * slope[...]).astype(BF16)
    sums[...] = matmul(pgs[...], win[...])

    chunk = 2 * LANES

    def weight_out():
        for i in range(width // chunk):
            lanes = slice(i * chunk, (i + 1) * chunk)
            wout_out[:, lanes] = matmul(act_t[...], grads[:, lanes]).astype(BF16)

    def transpose_pg():
        for i in range(pgs.shape[0] // LANES):
            rows = slice(i * LANES, (i + 1) * LANES)
            pg_t[:, rows] = pgs[rows, :].astype(F32).T.astype(BF16)

    def weight_in():
        for i in range(width // chunk):
            lanes = slice(i * chunk, (i + 1) * chunk)
            win_out[:, lanes] = matmul(pg_t[...], xp[:, lanes]).astype(BF16)

    give_sums(1, False)
    weight_out()
    transpose_pg()
    give_sums(1, True)
    give_sums(2, False)
    give_sums(2, True)
    give_sums(3, False)
    give_sums(3, True)
    weight_in()
    for r in range(ROW_PARTS):
        for h in range(2):
            for i in range(2):
                rs[3, r, h, i].wait_recv()
        got = slice(r * ALIGN, (r + 1) * ALIGN)
        total = sums[rows_part(y, r), :] + rs_in[3, 0, got, :].astype(F32) + rs_in[3, 1, got, :].astype(F32)
        total = total.astype(BF16).astype(F32)
        dot = jnp.sum(xp[rows_part(y, r), :].astype(F32) * total, axis=1, keepdims=True)
        dot_hi = dot.astype(BF16).astype(F32)
        columns = [total[:, i * LANES:(i + 1) * LANES] for i in range(cuts)]
        columns += [jnp.broadcast_to(v, (ALIGN, LANES)) for v in (dot_hi, dot - dot_hi)]
        first = place(r) * ALIGN
        for i in range(cuts // 2 + 1):
            out_b[pl.ds(first, ALIGN), i] = jnp.stack(columns[2 * i:2 * i + 2], axis=1).astype(BF16)

        @pl.loop(0, ALIGN)
        def _(n):
            t = first + (n + chip) % ALIGN

            @pl.when(t != me)
            def _():
                pltpu.make_async_remote_copy(
                    out_b.at[t], in_b.at[me], all_send.at[1], all_recv.at[1],
                    device_id=((t // CHIPS) * RING + y, 2 * (t % CHIPS) + core), device_id_type=MESH,
                ).start()

    self_b = pltpu.make_async_copy(out_b.at[me], in_b.at[me], all_self.at[1])
    self_b.start()
    pltpu.make_async_copy(in_b.at[all_but_one], in_b.at[all_but_one], all_recv.at[1]).wait()
    self_b.wait()

    for i in range(cuts // 2 + 1):
        v = in_b[:CHIPS, i].astype(F32) + in_b[CHIPS:, i].astype(F32)
        if i < cuts // 2:
            for k in range(2):
                back[mine, (2 * i + k) * LANES:(2 * i + k + 1) * LANES] = v[:, k]
        else:
            back[mine, width:width + LANES] = v[:, 0] + v[:, 1]
    send_back = pltpu.make_async_remote_copy(
        back.at[mine], back.at[mine], pair_send.at[2], pair_recv.at[2], device_id=other, device_id_type=MESH
    )
    send_back.start()
    send_back.wait_recv()

    send_part.wait_send()
    send_lse.wait_send()
    send_back.wait_send()
    for i, held in enumerate((in_a, in_b)):
        pltpu.make_async_copy(held.at[all_but_one], held.at[all_but_one], all_send.at[i]).wait()
    for copy in list(ag.values()) + list(rs.values()):
        copy.wait_send()


def finish(win_made, wout_made, tok, param_p, base, disp, back, tok_grad, win_grad, wout_grad, tok_out, sem):
    width = tok.shape[1]
    stores = [
        pltpu.make_async_copy(win_made, win_grad, sem.at[0]),
        pltpu.make_async_copy(wout_made, wout_grad, sem.at[1]),
    ]
    for store in stores:
        store.start()
    in_grad = back[:, :width].astype(BF16)
    disp_grad = matmul_t(in_grad, tok[...])
    logit_grad = base[...] + disp[...] * (disp_grad - back[:, width:width + LANES])
    left_t = jnp.concatenate([disp[...], logit_grad], axis=0).T.astype(BF16)
    half = width // 2
    for i in range(2):
        lanes = slice(i * half, (i + 1) * half)
        right_t = jnp.concatenate([in_grad[:, lanes], param_p[:, lanes]], axis=0)
        tok_out[:, lanes] = matmul(left_t, right_t).astype(BF16)
        store = pltpu.make_async_copy(tok_out.at[:, lanes], tok_grad.at[:, lanes], sem.at[2 + i])
        store.start()
        stores.append(store)
    for store in stores:
        store.wait()


def body(tokens, slot_param, out_grad, slot_outputs, slot_inputs, w_in, w_out):
    tok, ograd, sout = tokens[0], out_grad[0], slot_outputs[0]
    x = slot_inputs[:, 0]
    param = slot_param.T
    win, wout = w_in[0].T, w_out[0]
    images, width = x.shape
    hidden = wout.shape[0]
    slots = param.shape[0]
    tokens_here = tok.shape[0]
    pieces = width // (2 * LANES)
    vm = pltpu.VMEM
    dma = pltpu.SemaphoreType.DMA
    hbm = pl.BlockSpec(memory_space=pltpu.HBM)
    args = [pltpu.with_memory_space_constraint(v, pltpu.HBM) for v in (tok, param, ograd, sout, x, win, wout)]
    in_vmem = pl.BlockSpec(memory_space=pltpu.VMEM)
    made = pl.pallas_call(
        kernel,
        out_shape=(
            vm((hidden, width), BF16), vm((hidden, width), BF16), vm((tokens_here, width), BF16),
            vm((slots, width), BF16), vm((slots, LANES), F32), vm((slots, LANES), F32),
            vm((slots, width + LANES), F32),
        ),
        in_specs=[hbm] * 7,
        out_specs=(in_vmem,) * 7,
        scratch_shapes=[
            vm((slots, width), BF16), vm((tokens_here, width), BF16),
            vm((slots, width), BF16), vm((images, width), BF16), vm((hidden, width), BF16),
            vm((hidden, width), BF16),
            vm((images, width), BF16), vm((images, hidden), F32),
            vm((hidden, images), BF16), vm((images, width), BF16), vm((images, hidden), BF16),
            vm((hidden, images), BF16), vm((images, width), F32),
            vm((width // LANES, slots, LANES), F32), vm((width // LANES, CHIPS, LANES), F32),
            vm((slots, LANES), F32), vm((slots, LANES), F32),
            vm((CHIPS, pieces, 2, LANES), BF16), vm((BLOCK, pieces, 2, LANES), BF16),
            vm((BLOCK, pieces + 1, 2, LANES), BF16), vm((BLOCK, pieces + 1, 2, LANES), BF16),
            vm((4, 2, BLOCK, width), BF16), vm((4, 2, BLOCK, width), BF16),
            vm((width // LANES, CHIPS, LANES), F32),
            dma((7,)), dma((3,)), dma((3,)), dma((2,)), dma((2,)), dma((2,)),
            dma((4, 2, ROW_PARTS, 2)), dma((4, 2, ROW_PARTS, 2)), dma((4, 2, ROW_PARTS, 2)),
            dma((4, 2, ROW_PARTS, 2)),
        ],
        compiler_params=pltpu.CompilerParams(
            collective_id=0, has_side_effects=True, vmem_limit_bytes=40 * 1024 * 1024
        ),
    )(*args)
    tok_grad, win_grad, wout_grad = pl.pallas_call(
        finish,
        out_shape=(
            jax.ShapeDtypeStruct((tokens_here, width), BF16),
            jax.ShapeDtypeStruct((hidden, width), BF16),
            jax.ShapeDtypeStruct((hidden, width), BF16),
        ),
        in_specs=[in_vmem] * 7,
        out_specs=(hbm,) * 3,
        scratch_shapes=[vm((tokens_here, width), BF16), dma((4,))],
        compiler_params=pltpu.CompilerParams(vmem_limit_bytes=32 * 1024 * 1024),
    )(*made)
    return tok_grad[None], win_grad.T[None], wout_grad[None]


def solution(mesh):
    placed = (
        P(("dp", "expert"), None, None),
        P(),
        P(("dp", "expert"), None, None),
        P(("dp", "expert"), None, None),
        P(None, "expert", None),
        P("expert", None, "dp"),
        P("expert", "dp", None),
    )
    return jax.shard_map(
        body,
        mesh=mesh,
        in_specs=placed,
        out_specs=(
            P(("dp", "expert"), None, None),
            P("expert", None, "dp"),
            P("expert", "dp", None),
        ),
        check_vma=False,
    )
```
